512 devices in a mesh: dp: 32 (over z_lo, y), tensor: 16 (over x, z_hi, core).
Axes of the slice: x: 4, y: 8, z: 8 (z_hi: 2, z_lo: 4; z = z_hi * 4 + z_lo), core: 2. Of those that a mesh axis runs over, the one named last changes fastest.
Arguments:
- grads: bfloat16 [32, 1536, 16384], P('dp', None, 'tensor'), may hold values from -6 to 6
- projector: bfloat16 [16384, 512], P('tensor'), may hold values from -0.046875 to 0.046875
- weight: float32 [1536, 16384], P('dp', 'tensor'), may hold values from -0.1 to 0.1
- first_moment: float32 [1536, 512], P('dp', 'tensor'), may hold values from -0.2 to 0.2
- second_moment: float32 [1536, 512], P('dp', 'tensor'), may hold values from 1e-05 to 0.001
Outputs:
- new_weight: float32 [1536, 16384], P('dp', 'tensor')
- new_first: float32 [1536, 512], P('dp', 'tensor')
- new_second: float32 [1536, 512], P('dp', 'tensor')
The draws below stay inside these ranges and needn't reach their ends.
All inputs are finite; a program needn't handle non-finite values.
Results may differ from the reference program's by a relative error of at most 0.0016.
Values may be sent and summed in bfloat16 or wider, within the bound.
A program may use at most 64 MiB of HBM per device.

```python
import math
import jax
import jax.numpy as jnp
from jax import lax

ROWS = 16384
RANK = 512
COLS = 1536
N_DP = 32


def draw_projector(key, part):
    key = jax.random.fold_in(key, 3)
    key_base, key_level, key_shared, key_column = jax.random.split(key, 4)
    scale = ROWS ** (-0.5)
    base = jax.random.truncated_normal(key_base, -4.0, 4.0, (ROWS, RANK), jnp.float32) * scale
    level = jnp.exp(jax.random.uniform(key_level, (16,), jnp.float32, math.log(0.22), math.log(2.0)))
    shared = jax.random.truncated_normal(key_shared, -4.0, 4.0, (16, ROWS // 16), jnp.float32) * scale
    shared = (shared * level[:, None]).reshape(ROWS, 1)
    column_weights = jax.random.uniform(key_column, (1, RANK), jnp.float32, 0.9, 1.8) * RANK ** (-0.5)
    return jnp.clip(base + shared * column_weights, -6.0 * scale, 6.0 * scale).astype(jnp.bfloat16)


def draw_first_moment(key, part):
    key = jax.random.fold_in(key, 5)
    key_base, key_sign = jax.random.split(key, 2)
    signs = (jax.random.randint(key_sign, (COLS, 1), 0, 2) * 2 - 1).astype(jnp.float32)
    base = jax.random.truncated_normal(key_base, -5.0, 5.0, (COLS, RANK), jnp.float32) * 0.03
    offset = jnp.full((COLS, 1), 0.05, jnp.float32)
    return base + signs * offset


def raised(array, stream_key, source, target, blocks, factor):
    def block_of(axis_at):
        return (jnp.arange(array.shape[axis_at]) // (array.shape[axis_at] // blocks)).reshape((-1,) + (1,) * (array.ndim - 1 - axis_at))

    near = jax.random.permutation(stream_key, blocks)[block_of(target)]
    other_side = (block_of(target) + blocks // 2) % blocks
    return jnp.where((block_of(source) == near) | (block_of(source) == other_side), factor * array, array)


def levels(rng, extent, pieces, least, top_value):
    def one(position, parts):
        draws = jax.random.uniform(jax.random.fold_in(jax.random.fold_in(rng, 6), position), (parts,), jnp.float32, least / len(pieces), top_value / len(pieces))
        return jnp.repeat(jnp.exp(draws), extent[position] // parts).reshape((-1,) + (1,) * (len(extent) - position - 1))

    level = one(*pieces[0])
    for cut in pieces[1:]:
        level = level * one(*cut)
    return level


def noise(stream_key, dims, deviation, limit, shards=(), dtype=jnp.bfloat16):
    result = deviation * jax.random.normal(stream_key, dims, jnp.float32)
    if shards:
        result = result * levels(stream_key, dims, shards, -0.22, 0.18)
    return jnp.clip(result, -limit, limit).astype(dtype)


def heavy_noise(rng, dims, deviation, most, cuts, heavy, held_as=jnp.bfloat16):
    drawn = deviation * jax.random.normal(rng, dims, jnp.float32)
    if cuts:
        drawn = drawn * levels(rng, dims, cuts, -0.22, 0.18)
    return jnp.clip(raised(drawn, jax.random.fold_in(rng, 3), *heavy), -most, most).astype(held_as)


def setup_inputs(seed: int = 0) -> dict:
    seeds = jax.random.split(jax.random.key(seed), 6)
    grads = heavy_noise(seeds[0], (N_DP, COLS, ROWS), 1.0, 6.0, ((0, 32), (2, 16)), (0, 1, 32, 2.75))
    projector = draw_projector(jax.random.fold_in(seeds[5], 71), 0)
    weight = noise(seeds[2], (COLS, ROWS), 0.02, 0.1, ((0, 32), (1, 16)), jnp.float32)
    first_moment = draw_first_moment(jax.random.fold_in(seeds[5], 71), 0)
    second_moment = jnp.clip(jnp.exp(math.log(0.001) - 4.6051703 * jax.random.uniform(seeds[4], (COLS, RANK), jnp.float32) ** levels(seeds[4], (COLS, RANK), ((0, 32), (1, 16)), -0.2, 0.2)), 9.999999747378752e-06, 0.001)
    return {"grads": grads, "projector": projector, "weight": weight, "first_moment": first_moment, "second_moment": second_moment}


def reference(grads, projector, weight, first_moment, second_moment):

    def accumulate(total, replica):
        return (total + jnp.dot(replica, projector, preferred_element_type=jnp.float32), None)
    start = jnp.zeros((grads.shape[1], projector.shape[1]), jnp.float32)
    summed, _ = lax.scan(accumulate, start, grads)
    projected = summed / N_DP
    new_first = 0.9 * first_moment + 0.1 * projected
    new_second = 0.999 * second_moment + 0.001 * projected * projected
    direction = (new_first / (jnp.sqrt(new_second) + 1e-08)).astype(jnp.bfloat16)
    update = jnp.dot(direction, projector.T, preferred_element_type=jnp.float32)
    total_sq = jnp.sum(update * update)
    factor = jnp.minimum(1.0, 0.02 * jnp.sqrt(float(COLS * ROWS)) / (jnp.sqrt(total_sq) + 1e-06))
    new_weight = weight - factor * update
    return (new_weight, new_first, new_second)
```

```python
import jax
import jax.numpy as jnp
from jax import lax
from jax.experimental import pallas as pl
from jax.experimental.pallas import tpu as pltpu
from jax.sharding import PartitionSpec as P

MESH = pl.DeviceIdType.MESH
F32, BF16 = jnp.float32, jnp.bfloat16

NX, NY, NZ, NZLO = 4, 8, 8, 4
ROWS, HALF, COLS, TILE = 48, 24, 512, 128
DEPTH = 1024
CHUNK = NY * ROWS

CORE = [(0, 0, 0, 1)]
XS = [(d, 0, 0, 0) for d in range(1, NX)]
YS = [(0, d, 0, 0) for d in range(1, NY)]
ZS = [(0, 0, d, 0) for d in range(1, NZ)]
XC = [(d, 0, 0, k) for d in range(NX) for k in range(2) if (d, k) != (0, 0)]
HC = [(0, 0, h, k) for h in (0, 4) for k in range(2) if (h, k) != (0, 0)]
PARTNERS = list(dict.fromkeys(YS + ZS + HC + XC))


def kernel(
    grads, projector, weight, first, second,
    new_weight, new_first, new_second,
    gbuf, pbuf, ptbuf, wbuf, mom, acc, crecv, xsend, xrecv, ysend, yrecv, zown, zrecv,
    mrecv, pboth, dsend, dall, upd, ssend, sxrecv, syrecv, szrecv,
    lsem, core_s, core_r, x_s, x_r, y_s, y_r, z_s, z_r, m_s, m_r, d_s, d_r, p_s, p_r, s_s, s_r,
):
    dp, tensor = lax.axis_index("dp"), lax.axis_index("tensor")
    zlo, y = dp // NY, dp % NY
    x, zhi, core = tensor // 4, (tensor // 2) % 2, tensor % 2
    z = zhi * NZLO + zlo
    other = 1 - core
    quarter = zhi * 2 + core

    def at(delta):
        dx, dy, dz, dk = delta
        px, py, pz, pk = (x + dx) % NX, (y + dy) % NY, (z + dz) % NZ, (core + dk) % 2
        return ((pz % NZLO) * NY + py, px * 4 + (pz // NZLO) * 2 + pk)

    pending = []

    def send(src, dst, send_sem, recv_sem, delta):
        copy = pltpu.make_async_remote_copy(
            src_ref=src, dst_ref=dst, send_sem=send_sem, recv_sem=recv_sem,
            device_id=at(delta), device_id_type=MESH,
        )
        copy.start()
        pending.append(copy)
        return copy

    loads = [pltpu.make_async_copy(projector, pbuf, lsem.at[0])]
    for s in range(NZLO):
        chunk = (zlo + s + 1) % NZLO
        rows = pl.ds(pl.multiple_of(chunk * CHUNK, CHUNK), CHUNK)
        loads.append(pltpu.make_async_copy(grads.at[0, rows], gbuf.at[s], lsem.at[1 + s]))
    loads.append(pltpu.make_async_copy(first, mom.at[0], lsem.at[5]))
    loads.append(pltpu.make_async_copy(second, mom.at[1], lsem.at[6]))
    loads.append(pltpu.make_async_copy(weight, wbuf, lsem.at[7]))
    for load in loads:
        load.start()

    barrier = pltpu.get_barrier_semaphore()
    for delta in PARTNERS:
        pl.semaphore_signal(barrier, inc=1, device_id=at(delta), device_id_type=MESH)

    loads[0].wait()
    for s in range(NZLO):
        loads[1 + s].wait()

        @pl.loop(0, 2)
        def _(part):
            block = gbuf[s, pl.ds(pl.multiple_of(part * 192, 192), 192)]
            out = jnp.dot(block, pbuf[...], preferred_element_type=F32)
            acc[s, pl.ds(part * 4, 4)] = out.reshape(4, 2, HALF, COLS)

    ptbuf[...] = pbuf[...].T
    pl.semaphore_wait(barrier, len(PARTNERS))

    core_copies = [
        send(acc.at[s, :, other], crecv.at[s], core_s.at[s], core_r.at[s], CORE[0])
        for s in range(NZLO)
    ]
    loads[5].wait()
    loads[6].wait()
    m_copies = []
    for j, delta in enumerate(HC):
        target_half = (core + delta[3]) % 2
        rows = pl.ds(pl.multiple_of(target_half * HALF, 8), HALF)
        m_copies.append(send(mom.at[:, rows], mrecv.at[quarter], m_s.at[j], m_r.at[j], delta))
    mrecv[quarter] = mom[:, pl.ds(pl.multiple_of(core * HALF, 8), HALF)]

    x_copies = []
    for s in range(NZLO):
        core_copies[s].wait_recv()
        for j, delta in enumerate(XS):
            lanes = pl.ds(pl.multiple_of(((x + delta[0]) % NX) * TILE, TILE), TILE)
            tile = acc[s, :, core, :, lanes] + crecv[s, :, :, lanes]
            xsend[s, j] = tile.reshape(NY * HALF, TILE).astype(BF16)
            x_copies.append(send(xsend.at[s, j], xrecv.at[s, j], x_s.at[s, j], x_r.at[s, j], delta))

    y_copies = []
    for s in range(NZLO):
        for j in range(len(XS)):
            x_copies[s * len(XS) + j].wait_recv()
        lanes = pl.ds(pl.multiple_of(x * TILE, TILE), TILE)
        total = acc[s, :, core, :, lanes] + crecv[s, :, :, lanes]
        for j in range(len(XS)):
            total = total + xrecv[s, j].astype(F32).reshape(NY, HALF, TILE)
        ysend[s] = total
        for j, delta in enumerate(YS):
            y_copies.append(
                send(ysend.at[s, (y + delta[1]) % NY], yrecv.at[s, j], y_s.at[s, j], y_r.at[s, j], delta)
            )

    z_copies = {}
    for s in range(NZLO):
        for j in range(len(YS)):
            y_copies[s * len(YS) + j].wait_recv()
        total = ysend[s, y]
        for j in range(len(YS)):
            total = total + yrecv[s, j]
        zown[s] = total
        for d in (s + 1, s + 5):
            if d < NZ:
                z_copies[d] = send(zown.at[s], zrecv.at[d - 1], z_s.at[d - 1], z_r.at[d - 1], ZS[d - 1])

    for copy in m_copies:
        copy.wait_recv()
    m_first = jnp.concatenate([mrecv[q, 0] for q in range(4)], axis=1)
    m_second = jnp.concatenate([mrecv[q, 1] for q in range(4)], axis=1)
    total = zown[NZLO - 1]
    for d in range(1, NZ):
        z_copies[d].wait_recv()
        total = total + zrecv[d - 1]
    averaged = total * (1.0 / 32.0)

    def moments(old_first, old_second, mean):
        return 0.9 * old_first + 0.1 * mean, 0.999 * old_second + 0.001 * mean * mean

    f, v = moments(m_first, m_second, averaged)
    direction = f / (jnp.sqrt(v) + 1e-08)
    direction = jnp.concatenate([direction, jnp.zeros((8, TILE), F32)], axis=0).astype(BF16)
    dsend[...] = direction
    d_copies = []
    for j, delta in enumerate(XC):
        d_copies.append(send(dsend, dall.at[core, x], d_s.at[j], d_r.at[j], delta))
    pboth[core] = averaged
    p_copy = send(pboth.at[core], pboth.at[core], p_s, p_r, CORE[0])
    dall[core, x] = direction
    for copy in d_copies:
        copy.wait_recv()
    whole = jnp.concatenate(
        [jnp.concatenate([dall[k, t] for t in range(NX)], axis=1) for k in range(2)], axis=0
    )
    update = jnp.dot(whole, ptbuf[...], preferred_element_type=F32)
    update = jnp.concatenate([update[0:HALF], update[32:32 + HALF]], axis=0)
    upd[...] = update
    square = update * update
    folded = square[0:8]
    for r in range(1, ROWS // 8):
        folded = folded + square[8 * r:8 * r + 8]
    lanes_sum = folded[:, 0:TILE]
    for t in range(1, DEPTH // TILE):
        lanes_sum = lanes_sum + folded[:, t * TILE:(t + 1) * TILE]
    total = jnp.sum(lanes_sum, axis=0, keepdims=True)

    n = 0
    for r, (deltas, box) in enumerate(((XC, sxrecv), (YS, syrecv), (ZS, szrecv))):
        ssend[r] = total
        copies = []
        for j, delta in enumerate(deltas):
            copies.append(send(ssend.at[r], box.at[j], s_s.at[n], s_r.at[n], delta))
            n += 1
        if r == 0:
            p_copy.wait_recv()
            pieces = []
            for k in range(2):
                mean = pboth[k]
                piece = mean[:, 0:32]
                for q in range(1, 4):
                    piece = jnp.where(quarter == q, mean[:, 32 * q:32 * q + 32], piece)
                pieces.append(piece)
            f, v = moments(mom[0], mom[1], jnp.concatenate(pieces, axis=0))
            new_first[...] = f
            new_second[...] = v
            loads[7].wait()
        for j, copy in enumerate(copies):
            copy.wait_recv()
            total = total + box[j]

    total_sq = jnp.sum(total, axis=1, keepdims=True)
    entries = float(1536 * 16384)
    factor = jnp.minimum(1.0, 0.02 * entries**0.5 / (jnp.sqrt(total_sq) + 1e-06))
    new_weight[...] = wbuf[...] - factor * upd[...]
    for copy in pending:
        copy.wait_send()


def body(grads, projector, weight, first_moment, second_moment):
    sem = pltpu.SemaphoreType.DMA
    vm = pltpu.VMEM
    return pl.pallas_call(
        kernel,
        name="galore_step",
        out_shape=(
            jax.ShapeDtypeStruct((ROWS, DEPTH), F32),
            jax.ShapeDtypeStruct((ROWS, 32), F32),
            jax.ShapeDtypeStruct((ROWS, 32), F32),
        ),
        in_specs=[pl.BlockSpec(memory_space=pl.ANY)] * 5,
        out_specs=(pl.BlockSpec(memory_space=pltpu.VMEM),) * 3,
        scratch_shapes=[
            vm((NZLO, CHUNK, DEPTH), BF16),
            vm((DEPTH, COLS), BF16),
            vm((COLS, DEPTH), BF16),
            vm((ROWS, DEPTH), F32),
            vm((2, ROWS, 32), F32),
            vm((NZLO, NY, 2, HALF, COLS), F32),
            vm((NZLO, NY, HALF, COLS), F32),
            vm((NZLO, 3, NY * HALF, TILE), BF16),
            vm((NZLO, 3, NY * HALF, TILE), BF16),
            vm((NZLO, NY, HALF, TILE), F32),
            vm((NZLO, 7, HALF, TILE), F32),
            vm((NZLO, HALF, TILE), F32),
            vm((7, HALF, TILE), F32),
            vm((4, 2, HALF, 32), F32),
            vm((2, HALF, TILE), F32),
            vm((32, TILE), BF16),
            vm((2, NX, 32, TILE), BF16),
            vm((ROWS, DEPTH), F32),
            vm((3, 1, TILE), F32),
            vm((7, 1, TILE), F32),
            vm((7, 1, TILE), F32),
            vm((7, 1, TILE), F32),
            sem((8,)),
            sem((NZLO,)), sem((NZLO,)),
            sem((NZLO, 3)), sem((NZLO, 3)),
            sem((NZLO, 7)), sem((NZLO, 7)),
            sem((7,)), sem((7,)),
            sem((3,)), sem((3,)),
            sem((7,)), sem((7,)),
            sem, sem,
            sem((21,)), sem((21,)),
        ],
        compiler_params=pltpu.CompilerParams(
            collective_id=0, has_side_effects=True, vmem_limit_bytes=48 * 2**20
        ),
    )(grads, projector, weight, first_moment, second_moment)


def solution(mesh):
    placed = (
        P("dp", None, "tensor"),
        P("tensor", None),
        P("dp", "tensor"),
        P("dp", "tensor"),
        P("dp", "tensor"),
    )
    return jax.shard_map(
        body,
        mesh=mesh,
        in_specs=placed,
        out_specs=(P("dp", "tensor"), P("dp", "tensor"), P("dp", "tensor")),
        check_vma=False,
    )
```

```python
import jax
import jax.numpy as jnp
from jax import lax
from jax.experimental import pallas as pl
from jax.experimental.pallas import tpu as pltpu
from jax.sharding import PartitionSpec as P

MESH = pl.DeviceIdType.MESH
F32, BF16 = jnp.float32, jnp.bfloat16

NX, NY, NZ, NZLO = 4, 8, 8, 4
ROWS, HALF, COLS, TILE = 48, 24, 512, 128
DEPTH = 1024
CHUNK = NY * ROWS

CORE = [(0, 0, 0, 1)]
XS = [(d, 0, 0, 0) for d in range(1, NX)]
YS = [(0, d, 0, 0) for d in range(1, NY)]
ZS = [(0, 0, d, 0) for d in range(1, NZ)]
XC = [(d, 0, 0, k) for d in range(NX) for k in range(2) if (d, k) != (0, 0)]
HC = [(0, 0, h, k) for h in (0, 4) for k in range(2) if (h, k) != (0, 0)]
PARTNERS = list(dict.fromkeys(YS + ZS + HC + XC))


def flip(block):
    rows, cols = block.shape
    wide = jnp.concatenate([block, jnp.zeros((rows, 128 - cols), F32)], axis=1)
    square = jnp.concatenate([wide, jnp.zeros((128 - rows, 128), F32)], axis=0)
    return square.T[:cols, :rows]


def kernel(
    grads, projector, first, second,
    step, mean_t,
    gbuf, pbuf, ptbuf, mom_t, mom, acc, crecv, xsend, xrecv, ysend, yrecv, zown, zrecv,
    mrecv, pboth, dsend, dall, upd, ssend, sxrecv, syrecv, szrecv,
    lsem, core_s, core_r, x_s, x_r, y_s, y_r, z_s, z_r, m_s, m_r, d_s, d_r, p_s, p_r, s_s, s_r,
):
    dp, tensor = lax.axis_index("dp"), lax.axis_index("tensor")
    zlo, y = dp // NY, dp % NY
    x, zhi, core = tensor // 4, (tensor // 2) % 2, tensor % 2
    z = zhi * NZLO + zlo
    other = 1 - core
    quarter = zhi * 2 + core

    def at(delta):
        dx, dy, dz, dk = delta
        px, py, pz, pk = (x + dx) % NX, (y + dy) % NY, (z + dz) % NZ, (core + dk) % 2
        return ((pz % NZLO) * NY + py, px * 4 + (pz // NZLO) * 2 + pk)

    pending = []

    def send(src, dst, send_sem, recv_sem, delta):
        copy = pltpu.make_async_remote_copy(
            src_ref=src, dst_ref=dst, send_sem=send_sem, recv_sem=recv_sem,
            device_id=at(delta), device_id_type=MESH,
        )
        copy.start()
        pending.append(copy)
        return copy

    loads = [pltpu.make_async_copy(projector, pbuf, lsem.at[0])]
    for s in range(NZLO):
        chunk = (zlo + s + 1) % NZLO
        rows = pl.ds(pl.multiple_of(chunk * CHUNK, CHUNK), CHUNK)
        loads.append(pltpu.make_async_copy(grads.at[0, rows], gbuf.at[s], lsem.at[1 + s]))
    loads.append(pltpu.make_async_copy(first, mom_t.at[0], lsem.at[5]))
    loads.append(pltpu.make_async_copy(second, mom_t.at[1], lsem.at[6]))
    for load in loads:
        load.start()

    barrier = pltpu.get_barrier_semaphore()
    for delta in PARTNERS:
        pl.semaphore_signal(barrier, inc=1, device_id=at(delta), device_id_type=MESH)

    loads[5].wait()
    loads[6].wait()
    mom[0] = flip(mom_t[0])
    mom[1] = flip(mom_t[1])
    loads[0].wait()
    for s in range(NZLO):
        loads[1 + s].wait()
        out = jnp.dot(gbuf[s], pbuf[...], preferred_element_type=F32)
        acc[s] = out.reshape(NY, 2, HALF, COLS)

    ptbuf[...] = pbuf[...].T
    pl.semaphore_wait(barrier, len(PARTNERS))

    core_copies = [
        send(acc.at[s, :, other], crecv.at[s], core_s.at[s], core_r.at[s], CORE[0])
        for s in range(NZLO)
    ]
    m_copies = []
    for j, delta in enumerate(HC):
        target_half = (core + delta[3]) % 2
        rows = pl.ds(pl.multiple_of(target_half * HALF, 8), HALF)
        m_copies.append(send(mom.at[:, rows], mrecv.at[quarter], m_s.at[j], m_r.at[j], delta))
    mrecv[quarter] = mom[:, pl.ds(pl.multiple_of(core * HALF, 8), HALF)]

    x_copies = []
    for s in range(NZLO):
        core_copies[s].wait_recv()
        for j, delta in enumerate(XS):
            lanes = pl.ds(pl.multiple_of(((x + delta[0]) % NX) * TILE, TILE), TILE)
            tile = acc[s, :, core, :, lanes] + crecv[s, :, :, lanes]
            xsend[s, j] = tile.reshape(NY * HALF, TILE).astype(BF16)
            x_copies.append(send(xsend.at[s, j], xrecv.at[s, j], x_s.at[s, j], x_r.at[s, j], delta))

    y_copies = []
    for s in range(NZLO):
        for j in range(len(XS)):
            x_copies[s * len(XS) + j].wait_recv()
        lanes = pl.ds(pl.multiple_of(x * TILE, TILE), TILE)
        total = acc[s, :, core, :, lanes] + crecv[s, :, :, lanes]
        for j in range(len(XS)):
            total = total + xrecv[s, j].astype(F32).reshape(NY, HALF, TILE)
        ysend[s] = total
        for j, delta in enumerate(YS):
            y_copies.append(
                send(ysend.at[s, (y + delta[1]) % NY], yrecv.at[s, j], y_s.at[s, j], y_r.at[s, j], delta)
            )

    z_copies = {}
    for s in range(NZLO):
        for j in range(len(YS)):
            y_copies[s * len(YS) + j].wait_recv()
        total = ysend[s, y]
        for j in range(len(YS)):
            total = total + yrecv[s, j]
        zown[s] = total
        for d in (s + 1, s + 5):
            if d < NZ:
                z_copies[d] = send(zown.at[s], zrecv.at[d - 1], z_s.at[d - 1], z_r.at[d - 1], ZS[d - 1])

    for copy in m_copies:
        copy.wait_recv()
    m_first = jnp.concatenate([mrecv[q, 0] for q in range(4)], axis=1)
    m_second = jnp.concatenate([mrecv[q, 1] for q in range(4)], axis=1)
    total = zown[NZLO - 1]
    for d in range(1, NZ):
        z_copies[d].wait_recv()
        total = total + zrecv[d - 1]
    averaged = total * (1.0 / 32.0)

    def moments(old_first, old_second, mean):
        return 0.9 * old_first + 0.1 * mean, 0.999 * old_second + 0.001 * mean * mean

    f, v = moments(m_first, m_second, averaged)
    direction = f / (jnp.sqrt(v) + 1e-08)
    direction = jnp.concatenate([direction, jnp.zeros((8, TILE), F32)], axis=0).astype(BF16)
    dsend[...] = direction
    d_copies = []
    for j, delta in enumerate(XC):
        d_copies.append(send(dsend, dall.at[core, x], d_s.at[j], d_r.at[j], delta))
    pboth[core] = averaged
    p_copy = send(pboth.at[core], pboth.at[core], p_s, p_r, CORE[0])
    dall[core, x] = direction
    for copy in d_copies:
        copy.wait_recv()
    whole = jnp.concatenate(
        [jnp.concatenate([dall[k, t] for t in range(NX)], axis=1) for k in range(2)], axis=0
    )
    update = jnp.dot(whole, ptbuf[...], preferred_element_type=F32)
    update = jnp.concatenate([update[0:HALF], update[32:32 + HALF]], axis=0)
    upd[...] = update
    square = update * update
    folded = square[0:8]
    for r in range(1, ROWS // 8):
        folded = folded + square[8 * r:8 * r + 8]
    lanes_sum = folded[:, 0:TILE]
    for t in range(1, DEPTH // TILE):
        lanes_sum = lanes_sum + folded[:, t * TILE:(t + 1) * TILE]
    total = jnp.sum(lanes_sum, axis=0, keepdims=True)

    n = 0
    for r, (deltas, box) in enumerate(((XC, sxrecv), (YS, syrecv), (ZS, szrecv))):
        ssend[r] = total
        copies = []
        for j, delta in enumerate(deltas):
            copies.append(send(ssend.at[r], box.at[j], s_s.at[n], s_r.at[n], delta))
            n += 1
        if r == 0:
            p_copy.wait_recv()
            pieces = []
            for k in range(2):
                mean = pboth[k]
                piece = mean[:, 0:32]
                for q in range(1, 4):
                    piece = jnp.where(quarter == q, mean[:, 32 * q:32 * q + 32], piece)
                pieces.append(piece)
            mean_t[...] = flip(jnp.concatenate(pieces, axis=0))
        for j, copy in enumerate(copies):
            copy.wait_recv()
            total = total + box[j]

    total_sq = jnp.sum(total, axis=1, keepdims=True)
    entries = float(1536 * 16384)
    factor = jnp.minimum(1.0, 0.02 * entries**0.5 / (jnp.sqrt(total_sq) + 1e-06))
    step[...] = factor * upd[...]
    for copy in pending:
        copy.wait_send()


def body(grads, projector, weight, first_moment, second_moment):
    sem = pltpu.SemaphoreType.DMA
    vm = pltpu.VMEM
    operands = (grads, projector, first_moment.T, second_moment.T)
    step, mean_t = pl.pallas_call(
        kernel,
        name="galore_step",
        out_shape=(
            jax.ShapeDtypeStruct((ROWS, DEPTH), F32),
            jax.ShapeDtypeStruct((32, ROWS), F32),
        ),
        in_specs=[pl.BlockSpec(memory_space=pltpu.HBM)] * 4,
        out_specs=(pl.BlockSpec(memory_space=pltpu.VMEM),) * 2,
        scratch_shapes=[
            vm((NZLO, CHUNK, DEPTH), BF16),
            vm((DEPTH, COLS), BF16),
            vm((COLS, DEPTH), BF16),
            vm((2, 32, ROWS), F32),
            vm((2, ROWS, 32), F32),
            vm((NZLO, NY, 2, HALF, COLS), F32),
            vm((NZLO, NY, HALF, COLS), F32),
            vm((NZLO, 3, NY * HALF, TILE), BF16),
            vm((NZLO, 3, NY * HALF, TILE), BF16),
            vm((NZLO, NY, HALF, TILE), F32),
            vm((NZLO, 7, HALF, TILE), F32),
            vm((NZLO, HALF, TILE), F32),
            vm((7, HALF, TILE), F32),
            vm((4, 2, HALF, 32), F32),
            vm((2, HALF, TILE), F32),
            vm((32, TILE), BF16),
            vm((2, NX, 32, TILE), BF16),
            vm((ROWS, DEPTH), F32),
            vm((3, 1, TILE), F32),
            vm((7, 1, TILE), F32),
            vm((7, 1, TILE), F32),
            vm((7, 1, TILE), F32),
            sem((7,)),
            sem((NZLO,)), sem((NZLO,)),
            sem((NZLO, 3)), sem((NZLO, 3)),
            sem((NZLO, 7)), sem((NZLO, 7)),
            sem((7,)), sem((7,)),
            sem((3,)), sem((3,)),
            sem((7,)), sem((7,)),
            sem, sem,
            sem((21,)), sem((21,)),
        ],
        compiler_params=pltpu.CompilerParams(
            collective_id=0, has_side_effects=True, vmem_limit_bytes=48 * 2**20
        ),
    )(*(pltpu.with_memory_space_constraint(a, pltpu.HBM) for a in operands))
    mean = mean_t.T
    new_first = 0.9 * first_moment + 0.1 * mean
    new_second = 0.999 * second_moment + 0.001 * mean * mean
    return weight - step, new_first, new_second


def solution(mesh):
    placed = (
        P("dp", None, "tensor"),
        P("tensor", None),
        P("dp", "tensor"),
        P("dp", "tensor"),
        P("dp", "tensor"),
    )
    return jax.shard_map(
        body,
        mesh=mesh,
        in_specs=placed,
        out_specs=(P("dp", "tensor"), P("dp", "tensor"), P("dp", "tensor")),
        check_vma=False,
    )
```

```python
import jax
import jax.numpy as jnp
from jax import lax
from jax.experimental import pallas as pl
from jax.experimental.pallas import tpu as pltpu
from jax.sharding import PartitionSpec as P

MESH = pl.DeviceIdType.MESH
F32, BF16 = jnp.float32, jnp.bfloat16

NX, NY, NZ, NZLO = 4, 8, 8, 4
ROWS, HALF, COLS, TILE = 48, 24, 512, 128
DEPTH = 1024
CHUNK = NY * ROWS
GREET = 1
STRIPE = 64

CORE = [(0, 0, 0, 1)]
XS = [(d, 0, 0, 0) for d in range(1, NX)]
YS = [(0, d, 0, 0) for d in range(1, NY)]
ZS = [(0, 0, d, 0) for d in range(1, NZ)]
XC = [(d, 0, 0, k) for d in range(NX) for k in range(2) if (d, k) != (0, 0)]
HC = [(0, 0, h, k) for h in (0, 4) for k in range(2) if (h, k) != (0, 0)]
PARTNERS = list(dict.fromkeys(YS + ZS + HC + XC))


def flip(block):
    rows, cols = block.shape
    wide = jnp.concatenate([block, jnp.zeros((rows, 128 - cols), F32)], axis=1)
    square = jnp.concatenate([wide, jnp.zeros((128 - rows, 128), F32)], axis=0)
    return square.T[:cols, :rows]


def kernel(
    grads, projector, first, second,
    step, mean_t,
    gbuf, pbuf, ptbuf, mom_t, mom, acc, crecv, xsend, xrecv, ysend, yrecv, zown, zrecv,
    yfsend, yfrecv, xfsum, xfrecv, gram, gcsend, gcrecv, gsum, gxsend, gxrecv, gfull,
    mrecv, pboth, dsend, dall, upd, ssend, syrecv, szrecv,
    lsem, core_s, core_r, x_s, x_r, y_s, y_r, z_s, z_r, m_s, m_r, d_s, d_r, p_s, p_r, s_s, s_r,
    yf_s, yf_r, xf_s, xf_r, gc_s, gc_r, gx_s, gx_r, ga_s, ga_r, gb_s, gb_r,
):
    dp, tensor = lax.axis_index("dp"), lax.axis_index("tensor")
    zlo, y = dp // NY, dp % NY
    x, zhi, core = tensor // 4, (tensor // 2) % 2, tensor % 2
    z = zhi * NZLO + zlo
    other = 1 - core
    quarter = zhi * 2 + core

    def at(delta):
        dx, dy, dz, dk = delta
        px, py, pz, pk = (x + dx) % NX, (y + dy) % NY, (z + dz) % NZ, (core + dk) % 2
        return ((pz % NZLO) * NY + py, px * 4 + (pz // NZLO) * 2 + pk)

    pending = []

    def send(src, dst, send_sem, recv_sem, delta):
        copy = pltpu.make_async_remote_copy(
            src_ref=src, dst_ref=dst, send_sem=send_sem, recv_sem=recv_sem,
            device_id=at(delta), device_id_type=MESH,
        )
        copy.start()
        pending.append(copy)
        return copy

    loads = [pltpu.make_async_copy(projector, pbuf, lsem.at[0])]
    for s in range(NZLO):
        chunk = (zlo + s + 1) % NZLO
        rows = pl.ds(pl.multiple_of(chunk * CHUNK, CHUNK), CHUNK)
        loads.append(pltpu.make_async_copy(grads.at[0, rows], gbuf.at[s], lsem.at[1 + s]))
    loads.append(pltpu.make_async_copy(first, mom_t.at[0], lsem.at[5]))
    loads.append(pltpu.make_async_copy(second, mom_t.at[1], lsem.at[6]))
    for load in loads:
        load.start()

    barrier = pltpu.get_barrier_semaphore()
    for delta in PARTNERS:
        pl.semaphore_signal(barrier, inc=1, device_id=at(delta), device_id_type=MESH)

    loads[5].wait()
    loads[6].wait()
    mom[0] = flip(mom_t[0])
    mom[1] = flip(mom_t[1])
    loads[0].wait()
    core_copies = []

    def core_send(s):
        core_copies.append(
            send(acc.at[s, :, other], crecv.at[s], core_s.at[s], core_r.at[s], CORE[0])
        )

    for s in range(NZLO):
        loads[1 + s].wait()
        out = jnp.dot(gbuf[s], pbuf[...], preferred_element_type=F32)
        acc[s] = out.reshape(NY, 2, HALF, COLS)
        if s == GREET:
            pl.semaphore_wait(barrier, len(PARTNERS))
            for t in range(s):
                core_send(t)
        if s >= GREET:
            core_send(s)

    m_copies = []
    for j, delta in enumerate(HC):
        target_half = (core + delta[3]) % 2
        rows = pl.ds(pl.multiple_of(target_half * HALF, 8), HALF)
        m_copies.append(send(mom.at[:, rows], mrecv.at[quarter], m_s.at[j], m_r.at[j], delta))
    mrecv[quarter] = mom[:, pl.ds(pl.multiple_of(core * HALF, 8), HALF)]

    def stacked(block):
        return jnp.concatenate([block[:, t * TILE:(t + 1) * TILE] for t in range(NX)], axis=0)

    core_copies[0].wait_recv()
    yf_copies = []
    for j, delta in enumerate(YS):
        there = (y + delta[1]) % NY
        yfsend[j] = stacked(acc[0, there, core] + crecv[0, there]).astype(BF16)
        yf_copies.append(send(yfsend.at[j], yfrecv.at[j], yf_s.at[j], yf_r.at[j], delta))

    x_copies = {}
    for s in range(1, NZLO):
        core_copies[s].wait_recv()
        for j, delta in enumerate(XS):
            lanes = pl.ds(pl.multiple_of(((x + delta[0]) % NX) * TILE, TILE), TILE)
            tile = acc[s, :, core, :, lanes] + crecv[s, :, :, lanes]
            xsend[s - 1, j] = tile.reshape(NY * HALF, TILE).astype(BF16)
            x_copies[s, j] = send(
                xsend.at[s - 1, j], xrecv.at[s - 1, j], x_s.at[s - 1, j], x_r.at[s - 1, j], delta
            )

    gram[...] = lax.dot_general(
        pbuf[...], pbuf[...], (((0,), (0,)), ((), ())), preferred_element_type=F32
    ).reshape(2, COLS // 2, COLS)
    gcsend[...] = gram[other].astype(BF16)
    gc_copy = send(gcsend, gcrecv, gc_s, gc_r, CORE[0])
    ptbuf[...] = pbuf[...].T

    y_copies = {}
    xf_copies = []

    def along_y(s):
        for j in range(len(XS)):
            x_copies[s, j].wait_recv()
        lanes = pl.ds(pl.multiple_of(x * TILE, TILE), TILE)
        total = acc[s, :, core, :, lanes] + crecv[s, :, :, lanes]
        for j in range(len(XS)):
            total = total + xrecv[s - 1, j].astype(F32).reshape(NY, HALF, TILE)
        ysend[s - 1] = total
        for j, delta in enumerate(YS):
            y_copies[s, j] = send(
                ysend.at[s - 1, (y + delta[1]) % NY], yrecv.at[s - 1, j],
                y_s.at[s - 1, j], y_r.at[s - 1, j], delta,
            )

    def along_x_after():
        total = stacked(acc[0, y, core] + crecv[0, y])
        for j in range(len(YS)):
            yf_copies[j].wait_recv()
            total = total + yfrecv[j].astype(F32)
        xfsum[...] = total.reshape(NX, HALF, TILE)
        for j, delta in enumerate(XS):
            xf_copies.append(
                send(xfsum.at[(x + delta[0]) % NX], xfrecv.at[j], xf_s.at[j], xf_r.at[j], delta)
            )

    along_y(1)
    along_y(2)
    along_x_after()
    along_y(3)

    gc_copy.wait_recv()
    gsum[...] = (gram[core] + gcrecv[...].astype(F32)).reshape(NX, STRIPE, COLS)
    gx_copies = []
    for j, delta in enumerate(XS):
        gxsend[j] = gsum[(x + delta[0]) % NX].astype(BF16)
        gx_copies.append(send(gxsend.at[j], gxrecv.at[j], gx_s.at[j], gx_r.at[j], delta))

    z_copies = {}
    for s in (1, 0, 2, 3):
        if s == 0:
            total = xfsum[x]
            for j in range(len(XS)):
                xf_copies[j].wait_recv()
                total = total + xfrecv[j]
        else:
            total = ysend[s - 1, y]
            for j in range(len(YS)):
                y_copies[s, j].wait_recv()
                total = total + yrecv[s - 1, j]
        zown[s] = total
        for d in (s + 1, s + 5):
            if d < NZ:
                z_copies[d] = send(zown.at[s], zrecv.at[d - 1], z_s.at[d - 1], z_r.at[d - 1], ZS[d - 1])

    stripe = gsum[x]
    for j in range(len(XS)):
        gx_copies[j].wait_recv()
        stripe = stripe + gxrecv[j].astype(F32)
    gfull[core, x] = stripe.astype(BF16)
    ga_copies = []
    for j, delta in enumerate(XS):
        ga_copies.append(
            send(gfull.at[core, x], gfull.at[core, x], ga_s.at[j], ga_r.at[j], delta)
        )

    for copy in m_copies:
        copy.wait_recv()
    m_first = jnp.concatenate([mrecv[q, 0] for q in range(4)], axis=1)
    m_second = jnp.concatenate([mrecv[q, 1] for q in range(4)], axis=1)
    total = zown[NZLO - 1]
    for d in range(1, NZ):
        z_copies[d].wait_recv()
        total = total + zrecv[d - 1]
    averaged = total * (1.0 / 32.0)

    def moments(old_first, old_second, mean):
        return 0.9 * old_first + 0.1 * mean, 0.999 * old_second + 0.001 * mean * mean

    f, v = moments(m_first, m_second, averaged)
    direction = f / (jnp.sqrt(v) + 1e-08)
    direction = jnp.concatenate([direction, jnp.zeros((8, TILE), F32)], axis=0).astype(BF16)
    dsend[...] = direction
    d_copies = []
    for j, delta in enumerate(XC):
        d_copies.append(send(dsend, dall.at[core, x], d_s.at[j], d_r.at[j], delta))
    pboth[core] = averaged
    p_copy = send(pboth.at[core], pboth.at[core], p_s, p_r, CORE[0])
    dall[core, x] = direction
    for copy in ga_copies:
        copy.wait_recv()
    gb_copy = send(gfull.at[core], gfull.at[core], gb_s, gb_r, CORE[0])
    for copy in d_copies:
        copy.wait_recv()
    whole = jnp.concatenate(
        [jnp.concatenate([dall[k, t] for t in range(NX)], axis=1) for k in range(2)], axis=0
    )
    gb_copy.wait_recv()
    square = jnp.dot(whole, gfull[...].reshape(COLS, COLS), preferred_element_type=F32)
    square = square * whole.astype(F32)
    folded = square[0:8]
    for r in range(1, 8):
        folded = folded + square[8 * r:8 * r + 8]
    lanes_sum = folded[:, 0:TILE]
    for t in range(1, NX):
        lanes_sum = lanes_sum + folded[:, t * TILE:(t + 1) * TILE]
    total = jnp.sum(lanes_sum, axis=0, keepdims=True)

    n = 0
    for r, (deltas, box) in enumerate(((YS, syrecv), (ZS, szrecv))):
        ssend[r] = total
        copies = []
        for j, delta in enumerate(deltas):
            copies.append(send(ssend.at[r], box.at[j], s_s.at[n], s_r.at[n], delta))
            n += 1
        if r == 0:
            update = jnp.dot(whole, ptbuf[...], preferred_element_type=F32)
            upd[...] = jnp.concatenate([update[0:HALF], update[32:32 + HALF]], axis=0)
            p_copy.wait_recv()
            pieces = []
            for k in range(2):
                mean = pboth[k]
                piece = mean[:, 0:32]
                for q in range(1, 4):
                    piece = jnp.where(quarter == q, mean[:, 32 * q:32 * q + 32], piece)
                pieces.append(piece)
            mean_t[...] = flip(jnp.concatenate(pieces, axis=0))
        for j, copy in enumerate(copies):
            copy.wait_recv()
            total = total + box[j]

    total_sq = jnp.sum(total, axis=1, keepdims=True)
    entries = float(1536 * 16384)
    factor = jnp.minimum(1.0, 0.02 * entries**0.5 / (jnp.sqrt(total_sq) + 1e-06))
    step[...] = factor * upd[...]
    for copy in pending:
        copy.wait_send()


def body(grads, projector, weight, first_moment, second_moment):
    sem = pltpu.SemaphoreType.DMA
    vm = pltpu.VMEM
    operands = (grads, projector, first_moment.T, second_moment.T)
    step, mean_t = pl.pallas_call(
        kernel,
        name="galore_step",
        out_shape=(
            jax.ShapeDtypeStruct((ROWS, DEPTH), F32),
            jax.ShapeDtypeStruct((32, ROWS), F32),
        ),
        in_specs=[pl.BlockSpec(memory_space=pltpu.HBM)] * 4,
        out_specs=(pl.BlockSpec(memory_space=pltpu.VMEM),) * 2,
        scratch_shapes=[
            vm((NZLO, CHUNK, DEPTH), BF16),
            vm((DEPTH, COLS), BF16),
            vm((COLS, DEPTH), BF16),
            vm((2, 32, ROWS), F32),
            vm((2, ROWS, 32), F32),
            vm((NZLO, NY, 2, HALF, COLS), F32),
            vm((NZLO, NY, HALF, COLS), F32),
            vm((3, 3, NY * HALF, TILE), BF16),
            vm((3, 3, NY * HALF, TILE), BF16),
            vm((3, NY, HALF, TILE), F32),
            vm((3, 7, HALF, TILE), F32),
            vm((NZLO, HALF, TILE), F32),
            vm((7, HALF, TILE), F32),
            vm((7, NX * HALF, TILE), BF16),
            vm((7, NX * HALF, TILE), BF16),
            vm((NX, HALF, TILE), F32),
            vm((3, HALF, TILE), F32),
            vm((2, COLS // 2, COLS), F32),
            vm((COLS // 2, COLS), BF16),
            vm((COLS // 2, COLS), BF16),
            vm((NX, STRIPE, COLS), F32),
            vm((3, STRIPE, COLS), BF16),
            vm((3, STRIPE, COLS), BF16),
            vm((2, NX, STRIPE, COLS), BF16),
            vm((4, 2, HALF, 32), F32),
            vm((2, HALF, TILE), F32),
            vm((32, TILE), BF16),
            vm((2, NX, 32, TILE), BF16),
            vm((ROWS, DEPTH), F32),
            vm((2, 1, TILE), F32),
            vm((7, 1, TILE), F32),
            vm((7, 1, TILE), F32),
            sem((7,)),
            sem((NZLO,)), sem((NZLO,)),
            sem((3, 3)), sem((3, 3)),
            sem((3, 7)), sem((3, 7)),
            sem((7,)), sem((7,)),
            sem((3,)), sem((3,)),
            sem((7,)), sem((7,)),
            sem, sem,
            sem((14,)), sem((14,)),
            sem((7,)), sem((7,)),
            sem((3,)), sem((3,)),
            sem, sem,
            sem((3,)), sem((3,)),
            sem((3,)), sem((3,)),
            sem, sem,
        ],
        compiler_params=pltpu.CompilerParams(
            collective_id=0, has_side_effects=True, vmem_limit_bytes=48 * 2**20
        ),
    )(*(pltpu.with_memory_space_constraint(a, pltpu.HBM) for a in operands))
    mean = mean_t.T
    new_first = 0.9 * first_moment + 0.1 * mean
    new_second = 0.999 * second_moment + 0.001 * mean * mean
    return weight - step, new_first, new_second


def solution(mesh):
    placed = (
        P("dp", None, "tensor"),
        P("tensor", None),
        P("dp", "tensor"),
        P("dp", "tensor"),
        P("dp", "tensor"),
    )
    return jax.shard_map(
        body,
        mesh=mesh,
        in_specs=placed,
        out_specs=(P("dp", "tensor"), P("dp", "tensor"), P("dp", "tensor")),
        check_vma=False,
    )
```

```python
import jax
import jax.numpy as jnp
from jax import lax
from jax.experimental import pallas as pl
from jax.experimental.pallas import tpu as pltpu
from jax.sharding import PartitionSpec as P

MESH = pl.DeviceIdType.MESH
F32, BF16 = jnp.float32, jnp.bfloat16

NX, NY, NZ, NZLO = 4, 8, 8, 4
ROWS, HALF, COLS, TILE = 48, 24, 512, 128
DEPTH = 1024
CHUNK = NY * ROWS

G_CORE, G_X, G_XL, G_Y, G_Z, G_M, G_D, G_P, G_SY, G_SZ = 0, 4, 6, 8, 11, 12, 13, 14, 15, 16
G_YF, G_XF, G_GC, G_GX, G_GA, G_GB, GROUPS = 17, 18, 19, 20, 21, 22, 23
GREET = 1
YF = 1
XF = (0, 2)
OWNER = (0, 1, 3, 2)
LAST = NZLO - 1
PARTS = ((4, 3, 5, 6), (2, 1, 7, 0))
STRIPE = 64
PADDED = 32

CORE = [(0, 0, 0, 1)]


def hops(delta):
    return sum(min(d, n - d) for d, n in zip(delta, (NX, NY, NZ, 2)))


def farthest_first(deltas):
    return sorted(deltas, key=hops, reverse=True)


XS = farthest_first([(d, 0, 0, 0) for d in range(1, NX)])
YS = farthest_first([(0, d, 0, 0) for d in range(1, NY)])
ZS = farthest_first([(0, 0, d, 0) for d in range(1, NZ)])
XC = farthest_first([(d, 0, 0, k) for d in range(NX) for k in range(2) if (d, k) != (0, 0)])
HC = farthest_first([(0, 0, h, k) for h in (0, 4) for k in range(2) if (h, k) != (0, 0)])
PARTNERS = farthest_first(dict.fromkeys(YS + ZS + HC + XC))


def flip(block):
    rows, cols = block.shape
    wide = jnp.concatenate([block, jnp.zeros((rows, 128 - cols), F32)], axis=1)
    square = jnp.concatenate([wide, jnp.zeros((128 - rows, 128), F32)], axis=0)
    return square.T[:cols, :rows]


def kernel(
    grads, projector, first, second,
    step, mean_t,
    gbuf, pbuf, mom_t, mom, acc, crecv, xsend, xrecv, xlsend, xlrecv, ysum, ysend, yrecv, ylown, ylsend, zown, zrecv,
    yfsend, yfrecv, xfsum, xfrecv, gram, gcsend, gcrecv, gsum, gxsend, gxrecv, gfull,
    mrecv, pboth, dsend, dall, upd, ssend, syrecv, szrecv,
    lsem, send_sem, recv_sem,
):
    dp, tensor = lax.axis_index("dp"), lax.axis_index("tensor")
    zlo, y = dp // NY, dp % NY
    x, zhi, core = tensor // 4, (tensor // 2) % 2, tensor % 2
    z = zhi * NZLO + zlo
    other = 1 - core
    quarter = zhi * 2 + core

    def at(delta):
        dx, dy, dz, dk = delta
        px, py, pz, pk = (x + dx) % NX, (y + dy) % NY, (z + dz) % NZ, (core + dk) % 2
        return ((pz % NZLO) * NY + py, px * 4 + (pz // NZLO) * 2 + pk)

    started = {}

    def send(group, like, src, dst, delta):
        pltpu.make_async_remote_copy(
            src_ref=src, dst_ref=dst, send_sem=send_sem.at[group], recv_sem=recv_sem.at[group],
            device_id=at(delta), device_id_type=MESH,
        ).start()
        started[group] = like

    def arrived(group):
        like = started[group]
        pltpu.make_async_copy(like, like, recv_sem.at[group]).wait()

    def sent(groups):
        for group in groups:
            like = started[group]
            pltpu.make_async_copy(like, like, send_sem.at[group]).wait()

    loads = [pltpu.make_async_copy(projector, pbuf, lsem.at[0])]
    for s in range(NZLO):
        chunk = (zlo + OWNER[s]) % NZLO
        rows = pl.ds(pl.multiple_of(chunk * CHUNK, CHUNK), CHUNK)
        loads.append(pltpu.make_async_copy(grads.at[0, rows], gbuf.at[s], lsem.at[1 + s]))
    loads.append(pltpu.make_async_copy(first, mom_t.at[0], lsem.at[5]))
    loads.append(pltpu.make_async_copy(second, mom_t.at[1], lsem.at[6]))

    for load in loads[:2]:
        load.start()
    barrier = pltpu.get_barrier_semaphore()
    for delta in PARTNERS:
        pl.semaphore_signal(barrier, inc=1, device_id=at(delta), device_id_type=MESH)
    for load in loads[2:]:
        load.start()

    loads[0].wait()

    def core_send(s):
        send(G_CORE + s, crecv.at[s], acc.at[s, :, other], crecv.at[s], CORE[0])

    for s in range(NZLO):
        loads[1 + s].wait()
        out = jnp.dot(gbuf[s], pbuf[...], preferred_element_type=F32)
        acc[s] = out.reshape(NY, 2, HALF, COLS)
        if s == GREET:
            pl.semaphore_wait(barrier, len(PARTNERS))
            for t in range(s):
                core_send(t)
        if s >= GREET:
            core_send(s)

    def stacked(block):
        return jnp.concatenate([block[:, t * TILE:(t + 1) * TILE] for t in range(NX)], axis=0)

    def along_y_first():
        arrived(G_CORE + YF)
        for j, delta in enumerate(YS):
            there = (y + delta[1]) % NY
            yfsend[j] = stacked(acc[YF, there, core] + crecv[YF, there]).astype(BF16)
            send(G_YF, yfrecv, yfsend.at[j], yfrecv.at[j], delta)

    def along_x_first(s):
        i = XF.index(s)
        arrived(G_CORE + s)
        for j, delta in enumerate(XS):
            lanes = pl.ds(pl.multiple_of(((x + delta[0]) % NX) * TILE, TILE), TILE)
            tile = acc[s, :, core, :, lanes] + crecv[s, :, :, lanes]
            xsend[i, j] = tile.reshape(NY * HALF, TILE).astype(BF16)
            send(G_X + i, xrecv.at[i], xsend.at[i, j], xrecv.at[i, j], delta)

    def last_part(d, lanes):
        there = (y + d) % NY
        return acc[LAST, there, core, :, lanes] + crecv[LAST, there, :, lanes]

    def along_x_last(part):
        for j, delta in enumerate(XS):
            lanes = pl.ds(pl.multiple_of(((x + delta[0]) % NX) * TILE, TILE), TILE)
            block = jnp.concatenate([last_part(d, lanes) for d in PARTS[part]], axis=0)
            xlsend[part, j] = block.astype(BF16)
            send(G_XL + part, xlrecv.at[part], xlsend.at[part, j], xlrecv.at[part, j], delta)

    along_x_first(0)
    along_y_first()
    along_x_first(2)
    arrived(G_CORE + LAST)
    along_x_last(0)
    along_x_last(1)

    loads[5].wait()
    loads[6].wait()
    mom[0] = flip(mom_t[0])
    mom[1] = flip(mom_t[1])
    for j, delta in enumerate(HC):
        target_half = (core + delta[3]) % 2
        rows = pl.ds(pl.multiple_of(target_half * HALF, 8), HALF)
        send(G_M, mrecv.at[0:3], mom.at[:, rows], mrecv.at[quarter], delta)
    mrecv[quarter] = mom[:, pl.ds(pl.multiple_of(core * HALF, 8), HALF)]

    gram[...] = lax.dot_general(
        pbuf[...], pbuf[...], (((0,), (0,)), ((), ())), preferred_element_type=F32
    ).reshape(2, COLS // 2, COLS)
    gcsend[...] = gram[other].astype(BF16)
    send(G_GC, gcrecv, gcsend, gcrecv, CORE[0])

    def along_y(s):
        i = XF.index(s)
        arrived(G_X + i)
        lanes = pl.ds(pl.multiple_of(x * TILE, TILE), TILE)
        total = acc[s, :, core, :, lanes] + crecv[s, :, :, lanes]
        for j in range(len(XS)):
            total = total + xrecv[i, j].astype(F32).reshape(NY, HALF, TILE)
        ysum[i] = total
        padded = jnp.concatenate([total, jnp.zeros((NY, PADDED - HALF, TILE), F32)], axis=1)
        ysend[i] = padded.astype(BF16)
        for j, delta in enumerate(YS):
            send(G_Y + i, yrecv.at[i], ysend.at[i, (y + delta[1]) % NY], yrecv.at[i, j], delta)

    def along_x_after():
        total = stacked(acc[YF, y, core] + crecv[YF, y])
        arrived(G_YF)
        for j in range(len(YS)):
            total = total + yfrecv[j].astype(F32)
        xfsum[...] = total.reshape(NX, HALF, TILE)
        for j, delta in enumerate(XS):
            send(G_XF, xfrecv, xfsum.at[(x + delta[0]) % NX], xfrecv.at[j], delta)

    def along_y_last(part):
        lanes = pl.ds(pl.multiple_of(x * TILE, TILE), TILE)
        arrived(G_XL + part)
        others = xlrecv[part, 0].astype(F32)
        for j in range(1, len(XS)):
            others = others + xlrecv[part, j].astype(F32)
        for q, d in enumerate(PARTS[part]):
            total = last_part(d, lanes) + others[q * HALF:(q + 1) * HALF]
            if d == 0:
                ylown[...] = total
                continue
            j = YS.index((0, d, 0, 0))
            padded = jnp.concatenate([total, jnp.zeros((PADDED - HALF, TILE), F32)], axis=0)
            ylsend[j] = padded.astype(BF16)
            send(G_Y + 2, yrecv.at[2], ylsend.at[j], yrecv.at[2, j], YS[j])

    along_y(0)
    along_y(2)
    arrived(G_GC)
    gsum[...] = (gram[core] + gcrecv[...].astype(F32)).reshape(NX, STRIPE, COLS)
    for j, delta in enumerate(XS):
        gxsend[j] = gsum[(x + delta[0]) % NX].astype(BF16)
        send(G_GX, gxrecv, gxsend.at[j], gxrecv.at[j], delta)
    along_y_last(0)
    along_y_last(1)
    along_x_after()

    for s in range(NZLO):
        if s == YF:
            total = xfsum[x]
            arrived(G_XF)
            for j in range(len(XS)):
                total = total + xfrecv[j]
        else:
            i = 2 if s == LAST else XF.index(s)
            total = ylown[...] if s == LAST else ysum[i, y]
            arrived(G_Y + i)
            for j in range(len(YS)):
                total = total + yrecv[i, j, 0:HALF].astype(F32)
        zown[s] = total
        for d in (OWNER[s] + NZLO, OWNER[s]):
            if d > 0:
                send(G_Z, zrecv, zown.at[s], zrecv.at[d - 1], (0, 0, d, 0))

    stripe = gsum[x]
    arrived(G_GX)
    for j in range(len(XS)):
        stripe = stripe + gxrecv[j].astype(F32)
    gfull[core, x] = stripe.astype(BF16)
    for delta in XS:
        send(G_GA, gfull.at[core, 0:3], gfull.at[core, x], gfull.at[core, x], delta)

    arrived(G_M)
    m_first = jnp.concatenate([mrecv[q, 0] for q in range(4)], axis=1)
    m_second = jnp.concatenate([mrecv[q, 1] for q in range(4)], axis=1)
    total = zown[0]
    arrived(G_Z)
    for d in range(1, NZ):
        total = total + zrecv[d - 1]
    averaged = total * (1.0 / 32.0)

    def moments(old_first, old_second, mean):
        return 0.9 * old_first + 0.1 * mean, 0.999 * old_second + 0.001 * mean * mean

    f, v = moments(m_first, m_second, averaged)
    direction = f / (jnp.sqrt(v) + 1e-08)
    direction = jnp.concatenate([direction, jnp.zeros((8, TILE), F32)], axis=0).astype(BF16)
    dsend[...] = direction
    for delta in XC:
        send(G_D, dall.at[0:7], dsend, dall.at[core * NX + x], delta)
    pboth[core] = averaged
    send(G_P, pboth.at[core], pboth.at[core], pboth.at[core], CORE[0])
    dall[core * NX + x] = direction
    arrived(G_GA)
    send(G_GB, gfull.at[core], gfull.at[core], gfull.at[core], CORE[0])
    arrived(G_D)
    whole = jnp.concatenate(
        [jnp.concatenate([dall[k * NX + t] for t in range(NX)], axis=1) for k in range(2)], axis=0
    )
    arrived(G_GB)
    square = jnp.dot(whole, gfull[...].reshape(COLS, COLS), preferred_element_type=F32)
    square = square * whole.astype(F32)
    folded = square[0:8]
    for r in range(1, 8):
        folded = folded + square[8 * r:8 * r + 8]
    lanes_sum = folded[:, 0:TILE]
    for t in range(1, NX):
        lanes_sum = lanes_sum + folded[:, t * TILE:(t + 1) * TILE]
    total = jnp.sum(lanes_sum, axis=0, keepdims=True)

    for r, (group, deltas, box) in enumerate(((G_SY, YS, syrecv), (G_SZ, ZS, szrecv))):
        ssend[r] = total
        for j, delta in enumerate(deltas):
            send(group, box, ssend.at[r], box.at[j], delta)
        if r == 0:
            update = lax.dot_general(
                whole, pbuf[...], (((1,), (1,)), ((), ())), preferred_element_type=F32
            )
            upd[...] = jnp.concatenate([update[0:HALF], update[32:32 + HALF]], axis=0)
            arrived(G_P)
            pieces = []
            for k in range(2):
                mean = pboth[k]
                piece = mean[:, 0:32]
                for q in range(1, 4):
                    piece = jnp.where(quarter == q, mean[:, 32 * q:32 * q + 32], piece)
                pieces.append(piece)
            mean_t[...] = flip(jnp.concatenate(pieces, axis=0))
            sent(g for g in range(GROUPS) if g not in (G_SY, G_SZ))
        arrived(group)
        for j in range(len(deltas)):
            total = total + box[j]

    total_sq = jnp.maximum(jnp.sum(total, axis=1, keepdims=True), 0.0)
    entries = float(1536 * 16384)
    factor = jnp.minimum(1.0, 0.02 * entries**0.5 / (jnp.sqrt(total_sq) + 1e-06))
    step[...] = factor * upd[...]
    sent((G_SY, G_SZ))


def body(grads, projector, weight, first_moment, second_moment):
    sem = pltpu.SemaphoreType.DMA
    vm = pltpu.VMEM
    operands = (grads, projector, first_moment.T, second_moment.T)
    step, mean_t = pl.pallas_call(
        kernel,
        name="galore_step",
        out_shape=(
            jax.ShapeDtypeStruct((ROWS, DEPTH), F32),
            jax.ShapeDtypeStruct((32, ROWS), F32),
        ),
        in_specs=[pl.BlockSpec(memory_space=pltpu.HBM)] * 4,
        out_specs=(pl.BlockSpec(memory_space=pltpu.VMEM),) * 2,
        scratch_shapes=[
            vm((NZLO, CHUNK, DEPTH), BF16),
            vm((DEPTH, COLS), BF16),
            vm((2, 32, ROWS), F32),
            vm((2, ROWS, 32), F32),
            vm((NZLO, NY, 2, HALF, COLS), F32),
            vm((NZLO, NY, HALF, COLS), F32),
            vm((2, 3, NY * HALF, TILE), BF16),
            vm((2, 3, NY * HALF, TILE), BF16),
            vm((2, 3, NY * HALF // 2, TILE), BF16),
            vm((2, 3, NY * HALF // 2, TILE), BF16),
            vm((2, NY, HALF, TILE), F32),
            vm((2, NY, PADDED, TILE), BF16),
            vm((3, 7, PADDED, TILE), BF16),
            vm((HALF, TILE), F32),
            vm((7, PADDED, TILE), BF16),
            vm((NZLO, HALF, TILE), F32),
            vm((7, HALF, TILE), F32),
            vm((7, NX * HALF, TILE), BF16),
            vm((7, NX * HALF, TILE), BF16),
            vm((NX, HALF, TILE), F32),
            vm((3, HALF, TILE), F32),
            vm((2, COLS // 2, COLS), F32),
            vm((COLS // 2, COLS), BF16),
            vm((COLS // 2, COLS), BF16),
            vm((NX, STRIPE, COLS), F32),
            vm((3, STRIPE, COLS), BF16),
            vm((3, STRIPE, COLS), BF16),
            vm((2, NX, STRIPE, COLS), BF16),
            vm((4, 2, HALF, 32), F32),
            vm((2, HALF, TILE), F32),
            vm((32, TILE), BF16),
            vm((2 * NX, 32, TILE), BF16),
            vm((ROWS, DEPTH), F32),
            vm((2, 1, TILE), F32),
            vm((7, 1, TILE), F32),
            vm((7, 1, TILE), F32),
            sem((7,)),
            sem((GROUPS,)),
            sem((GROUPS,)),
        ],
        compiler_params=pltpu.CompilerParams(
            collective_id=0, has_side_effects=True, vmem_limit_bytes=48 * 2**20
        ),
    )(*(pltpu.with_memory_space_constraint(a, pltpu.HBM) for a in operands))
    mean = mean_t.T
    new_first = 0.9 * first_moment + 0.1 * mean
    new_second = 0.999 * second_moment + 0.001 * mean * mean
    return weight - step, new_first, new_second


def solution(mesh):
    placed = (
        P("dp", None, "tensor"),
        P("tensor", None),
        P("dp", "tensor"),
        P("dp", "tensor"),
        P("dp", "tensor"),
    )
    return jax.shard_map(
        body,
        mesh=mesh,
        in_specs=placed,
        out_specs=(P("dp", "tensor"), P("dp", "tensor"), P("dp", "tensor")),
        check_vma=False,
    )
```

```python
import jax
import jax.numpy as jnp
from jax import lax
from jax.experimental import pallas as pl
from jax.experimental.pallas import tpu as pltpu
from jax.sharding import PartitionSpec as P

MESH = pl.DeviceIdType.MESH
F32, BF16 = jnp.float32, jnp.bfloat16

NX, NY, NZ, NZLO = 4, 8, 8, 4
ROWS, HALF, COLS, TILE = 48, 24, 512, 128
DEPTH = 1024
CHUNK = NY * ROWS

G_CORE, G_X, G_XL, G_Y, G_Z, G_M, G_D, G_P, G_S = 0, 4, 6, 8, 11, 12, 13, 14, 15
G_YF, G_XF, G_GC, G_GX, G_GA, G_GB, GROUPS = 16, 17, 18, 19, 20, 21, 22
GREET = 1
YF = 1
XF = (0, 2)
OWNER = (0, 1, 3, 2)
LAST = NZLO - 1
PARTS = ((4, 3, 5, 6), (2, 1, 7, 0))
STRIPE = 64
PADDED = 32

CORE = [(0, 0, 0, 1)]


def hops(delta):
    return sum(min(d, n - d) for d, n in zip(delta, (NX, NY, NZ, 2)))


def farthest_first(deltas):
    return sorted(deltas, key=hops, reverse=True)


XS = farthest_first([(d, 0, 0, 0) for d in range(1, NX)])
YS = farthest_first([(0, d, 0, 0) for d in range(1, NY)])
ZS = farthest_first([(0, 0, d, 0) for d in range(1, NZ)])
XC = farthest_first([(d, 0, 0, k) for d in range(NX) for k in range(2) if (d, k) != (0, 0)])
YZ = farthest_first([(0, a, b, 0) for a in range(NY) for b in range(NZ) if (a, b) != (0, 0)])
HC = farthest_first([(0, 0, h, k) for h in (0, 4) for k in range(2) if (h, k) != (0, 0)])
PARTNERS = farthest_first(dict.fromkeys(YS + ZS + HC + XC))


def flip(block):
    rows, cols = block.shape
    wide = jnp.concatenate([block, jnp.zeros((rows, 128 - cols), F32)], axis=1)
    square = jnp.concatenate([wide, jnp.zeros((128 - rows, 128), F32)], axis=0)
    return square.T[:cols, :rows]


def kernel(
    grads, projector, first, second,
    step, mean_t,
    gbuf, pbuf, mom_t, mom, acc, crecv, xsend, xrecv, xlsend, xlrecv, ysum, ysend, yrecv, ylown, ylsend, zown, zrecv,
    yfsend, yfrecv, xfsum, xfrecv, gram, gcsend, gcrecv, gsum, gxsend, gxrecv, gfull,
    mrecv, pboth, dsend, dall, upd, sown, sbox,
    lsem, send_sem, recv_sem,
):
    dp, tensor = lax.axis_index("dp"), lax.axis_index("tensor")
    zlo, y = dp // NY, dp % NY
    x, zhi, core = tensor // 4, (tensor // 2) % 2, tensor % 2
    z = zhi * NZLO + zlo
    other = 1 - core
    quarter = zhi * 2 + core

    def at(delta):
        dx, dy, dz, dk = delta
        px, py, pz, pk = (x + dx) % NX, (y + dy) % NY, (z + dz) % NZ, (core + dk) % 2
        return ((pz % NZLO) * NY + py, px * 4 + (pz // NZLO) * 2 + pk)

    started = {}

    def send(group, like, src, dst, delta):
        pltpu.make_async_remote_copy(
            src_ref=src, dst_ref=dst, send_sem=send_sem.at[group], recv_sem=recv_sem.at[group],
            device_id=at(delta), device_id_type=MESH,
        ).start()
        started[group] = like

    def arrived(group):
        like = started[group]
        pltpu.make_async_copy(like, like, recv_sem.at[group]).wait()

    def sent(groups):
        for group in groups:
            like = started[group]
            pltpu.make_async_copy(like, like, send_sem.at[group]).wait()

    loads = [pltpu.make_async_copy(projector, pbuf, lsem.at[0])]
    for s in range(NZLO):
        chunk = (zlo + OWNER[s]) % NZLO
        rows = pl.ds(pl.multiple_of(chunk * CHUNK, CHUNK), CHUNK)
        loads.append(pltpu.make_async_copy(grads.at[0, rows], gbuf.at[s], lsem.at[1 + s]))
    loads.append(pltpu.make_async_copy(first, mom_t.at[0], lsem.at[5]))
    loads.append(pltpu.make_async_copy(second, mom_t.at[1], lsem.at[6]))

    for load in loads[:2]:
        load.start()
    barrier = pltpu.get_barrier_semaphore()
    for delta in PARTNERS:
        pl.semaphore_signal(barrier, inc=1, device_id=at(delta), device_id_type=MESH)
    for load in loads[2:]:
        load.start()

    loads[0].wait()

    def core_send(s):
        send(G_CORE + s, crecv.at[s], acc.at[s, :, other], crecv.at[s], CORE[0])

    for s in range(NZLO):
        loads[1 + s].wait()
        out = jnp.dot(gbuf[s], pbuf[...], preferred_element_type=F32)
        acc[s] = out.reshape(NY, 2, HALF, COLS)
        if s == GREET:
            pl.semaphore_wait(barrier, len(PARTNERS))
            for t in range(s):
                core_send(t)
        if s >= GREET:
            core_send(s)

    def stacked(block):
        return jnp.concatenate([block[:, t * TILE:(t + 1) * TILE] for t in range(NX)], axis=0)

    def along_y_first():
        arrived(G_CORE + YF)
        for j, delta in enumerate(YS):
            there = (y + delta[1]) % NY
            yfsend[j] = stacked(acc[YF, there, core] + crecv[YF, there]).astype(BF16)
            send(G_YF, yfrecv, yfsend.at[j], yfrecv.at[j], delta)

    def along_x_first(s):
        i = XF.index(s)
        arrived(G_CORE + s)
        for j, delta in enumerate(XS):
            lanes = pl.ds(pl.multiple_of(((x + delta[0]) % NX) * TILE, TILE), TILE)
            tile = acc[s, :, core, :, lanes] + crecv[s, :, :, lanes]
            xsend[i, j] = tile.reshape(NY * HALF, TILE).astype(BF16)
            send(G_X + i, xrecv.at[i], xsend.at[i, j], xrecv.at[i, j], delta)

    def last_part(d, lanes):
        there = (y + d) % NY
        return acc[LAST, there, core, :, lanes] + crecv[LAST, there, :, lanes]

    def along_x_last(part):
        for j, delta in enumerate(XS):
            lanes = pl.ds(pl.multiple_of(((x + delta[0]) % NX) * TILE, TILE), TILE)
            block = jnp.concatenate([last_part(d, lanes) for d in PARTS[part]], axis=0)
            xlsend[part, j] = block.astype(BF16)
            send(G_XL + part, xlrecv.at[part], xlsend.at[part, j], xlrecv.at[part, j], delta)

    along_x_first(0)
    along_y_first()
    along_x_first(2)
    arrived(G_CORE + LAST)
    along_x_last(0)
    along_x_last(1)

    loads[5].wait()
    loads[6].wait()
    mom[0] = flip(mom_t[0])
    mom[1] = flip(mom_t[1])
    for j, delta in enumerate(HC):
        target_half = (core + delta[3]) % 2
        rows = pl.ds(pl.multiple_of(target_half * HALF, 8), HALF)
        send(G_M, mrecv.at[0:3], mom.at[:, rows], mrecv.at[quarter], delta)
    mrecv[quarter] = mom[:, pl.ds(pl.multiple_of(core * HALF, 8), HALF)]

    gram[...] = lax.dot_general(
        pbuf[...], pbuf[...], (((0,), (0,)), ((), ())), preferred_element_type=F32
    ).reshape(2, COLS // 2, COLS)
    gcsend[...] = gram[other].astype(BF16)
    send(G_GC, gcrecv, gcsend, gcrecv, CORE[0])

    def along_y(s):
        i = XF.index(s)
        arrived(G_X + i)
        lanes = pl.ds(pl.multiple_of(x * TILE, TILE), TILE)
        total = acc[s, :, core, :, lanes] + crecv[s, :, :, lanes]
        for j in range(len(XS)):
            total = total + xrecv[i, j].astype(F32).reshape(NY, HALF, TILE)
        ysum[i] = total
        padded = jnp.concatenate([total, jnp.zeros((NY, PADDED - HALF, TILE), F32)], axis=1)
        ysend[i] = padded.astype(BF16)
        for j, delta in enumerate(YS):
            send(G_Y + i, yrecv.at[i], ysend.at[i, (y + delta[1]) % NY], yrecv.at[i, j], delta)

    def along_x_after():
        total = stacked(acc[YF, y, core] + crecv[YF, y])
        arrived(G_YF)
        for j in range(len(YS)):
            total = total + yfrecv[j].astype(F32)
        xfsum[...] = total.reshape(NX, HALF, TILE)
        for j, delta in enumerate(XS):
            send(G_XF, xfrecv, xfsum.at[(x + delta[0]) % NX], xfrecv.at[j], delta)

    def along_y_last(part):
        lanes = pl.ds(pl.multiple_of(x * TILE, TILE), TILE)
        arrived(G_XL + part)
        others = xlrecv[part, 0].astype(F32)
        for j in range(1, len(XS)):
            others = others + xlrecv[part, j].astype(F32)
        for q, d in enumerate(PARTS[part]):
            total = last_part(d, lanes) + others[q * HALF:(q + 1) * HALF]
            if d == 0:
                ylown[...] = total
                continue
            j = YS.index((0, d, 0, 0))
            padded = jnp.concatenate([total, jnp.zeros((PADDED - HALF, TILE), F32)], axis=0)
            ylsend[j] = padded.astype(BF16)
            send(G_Y + 2, yrecv.at[2], ylsend.at[j], yrecv.at[2, j], YS[j])

    along_y(0)
    along_y(2)
    arrived(G_GC)
    gsum[...] = (gram[core] + gcrecv[...].astype(F32)).reshape(NX, STRIPE, COLS)
    for j, delta in enumerate(XS):
        gxsend[j] = gsum[(x + delta[0]) % NX].astype(BF16)
        send(G_GX, gxrecv, gxsend.at[j], gxrecv.at[j], delta)
    along_y_last(0)
    along_y_last(1)
    along_x_after()

    for s in range(NZLO):
        if s == YF:
            total = xfsum[x]
            arrived(G_XF)
            for j in range(len(XS)):
                total = total + xfrecv[j]
        else:
            i = 2 if s == LAST else XF.index(s)
            total = ylown[...] if s == LAST else ysum[i, y]
            arrived(G_Y + i)
            for j in range(len(YS)):
                total = total + yrecv[i, j, 0:HALF].astype(F32)
        zown[s] = total
        for d in (OWNER[s] + NZLO, OWNER[s]):
            if d > 0:
                send(G_Z, zrecv, zown.at[s], zrecv.at[d - 1], (0, 0, d, 0))

    stripe = gsum[x]
    arrived(G_GX)
    for j in range(len(XS)):
        stripe = stripe + gxrecv[j].astype(F32)
    gfull[core, x] = stripe.astype(BF16)
    for delta in XS:
        send(G_GA, gfull.at[core, 0:3], gfull.at[core, x], gfull.at[core, x], delta)

    arrived(G_M)
    m_first = jnp.concatenate([mrecv[q, 0] for q in range(4)], axis=1)
    m_second = jnp.concatenate([mrecv[q, 1] for q in range(4)], axis=1)
    total = zown[0]
    arrived(G_Z)
    for d in range(1, NZ):
        total = total + zrecv[d - 1]
    averaged = total * (1.0 / 32.0)

    def moments(old_first, old_second, mean):
        return 0.9 * old_first + 0.1 * mean, 0.999 * old_second + 0.001 * mean * mean

    f, v = moments(m_first, m_second, averaged)
    direction = f / (jnp.sqrt(v) + 1e-08)
    direction = jnp.concatenate([direction, jnp.zeros((8, TILE), F32)], axis=0).astype(BF16)
    dsend[...] = direction
    for delta in XC:
        send(G_D, dall.at[0:7], dsend, dall.at[core * NX + x], delta)
    pboth[core] = averaged
    send(G_P, pboth.at[core], pboth.at[core], pboth.at[core], CORE[0])
    dall[core * NX + x] = direction
    arrived(G_GA)
    send(G_GB, gfull.at[core], gfull.at[core], gfull.at[core], CORE[0])
    arrived(G_D)
    whole = jnp.concatenate(
        [jnp.concatenate([dall[k * NX + t] for t in range(NX)], axis=1) for k in range(2)], axis=0
    )
    arrived(G_GB)
    square = jnp.dot(whole, gfull[...].reshape(COLS, COLS), preferred_element_type=F32)
    square = square * whole.astype(F32)
    folded = square[0:8]
    for r in range(1, 8):
        folded = folded + square[8 * r:8 * r + 8]
    lanes_sum = folded[:, 0:TILE]
    for t in range(1, NX):
        lanes_sum = lanes_sum + folded[:, t * TILE:(t + 1) * TILE]
    total = jnp.sum(lanes_sum, axis=0, keepdims=True)

    sown[...] = total
    for j, delta in enumerate(YZ):
        send(G_S, sbox, sown, sbox.at[j], delta)
    update = lax.dot_general(
        whole, pbuf[...], (((1,), (1,)), ((), ())), preferred_element_type=F32
    )
    upd[...] = jnp.concatenate([update[0:HALF], update[32:32 + HALF]], axis=0)
    arrived(G_P)
    pieces = []
    for k in range(2):
        mean = pboth[k]
        piece = mean[:, 0:32]
        for q in range(1, 4):
            piece = jnp.where(quarter == q, mean[:, 32 * q:32 * q + 32], piece)
        pieces.append(piece)
    mean_t[...] = flip(jnp.concatenate(pieces, axis=0))
    sent(g for g in range(GROUPS) if g != G_S)
    arrived(G_S)
    total = total + jnp.sum(sbox[...], axis=0)

    total_sq = jnp.maximum(jnp.sum(total, axis=1, keepdims=True), 0.0)
    entries = float(1536 * 16384)
    factor = jnp.minimum(1.0, 0.02 * entries**0.5 / (jnp.sqrt(total_sq) + 1e-06))
    step[...] = factor * upd[...]
    sent((G_S,))


def body(grads, projector, weight, first_moment, second_moment):
    sem = pltpu.SemaphoreType.DMA
    vm = pltpu.VMEM
    operands = (grads, projector, first_moment.T, second_moment.T)
    step, mean_t = pl.pallas_call(
        kernel,
        name="galore_step",
        out_shape=(
            jax.ShapeDtypeStruct((ROWS, DEPTH), F32),
            jax.ShapeDtypeStruct((32, ROWS), F32),
        ),
        in_specs=[pl.BlockSpec(memory_space=pltpu.HBM)] * 4,
        out_specs=(pl.BlockSpec(memory_space=pltpu.VMEM),) * 2,
        scratch_shapes=[
            vm((NZLO, CHUNK, DEPTH), BF16),
            vm((DEPTH, COLS), BF16),
            vm((2, 32, ROWS), F32),
            vm((2, ROWS, 32), F32),
            vm((NZLO, NY, 2, HALF, COLS), F32),
            vm((NZLO, NY, HALF, COLS), F32),
            vm((2, 3, NY * HALF, TILE), BF16),
            vm((2, 3, NY * HALF, TILE), BF16),
            vm((2, 3, NY * HALF // 2, TILE), BF16),
            vm((2, 3, NY * HALF // 2, TILE), BF16),
            vm((2, NY, HALF, TILE), F32),
            vm((2, NY, PADDED, TILE), BF16),
            vm((3, 7, PADDED, TILE), BF16),
            vm((HALF, TILE), F32),
            vm((7, PADDED, TILE), BF16),
            vm((NZLO, HALF, TILE), F32),
            vm((7, HALF, TILE), F32),
            vm((7, NX * HALF, TILE), BF16),
            vm((7, NX * HALF, TILE), BF16),
            vm((NX, HALF, TILE), F32),
            vm((3, HALF, TILE), F32),
            vm((2, COLS // 2, COLS), F32),
            vm((COLS // 2, COLS), BF16),
            vm((COLS // 2, COLS), BF16),
            vm((NX, STRIPE, COLS), F32),
            vm((3, STRIPE, COLS), BF16),
            vm((3, STRIPE, COLS), BF16),
            vm((2, NX, STRIPE, COLS), BF16),
            vm((4, 2, HALF, 32), F32),
            vm((2, HALF, TILE), F32),
            vm((32, TILE), BF16),
            vm((2 * NX, 32, TILE), BF16),
            vm((ROWS, DEPTH), F32),
            vm((1, TILE), F32),
            vm((NY * NZ - 1, 1, TILE), F32),
            sem((7,)),
            sem((GROUPS,)),
            sem((GROUPS,)),
        ],
        compiler_params=pltpu.CompilerParams(
            collective_id=0, has_side_effects=True, vmem_limit_bytes=48 * 2**20
        ),
    )(*(pltpu.with_memory_space_constraint(a, pltpu.HBM) for a in operands))
    mean = mean_t.T
    new_first = 0.9 * first_moment + 0.1 * mean
    new_second = 0.999 * second_moment + 0.001 * mean * mean
    return weight - step, new_first, new_second


def solution(mesh):
    placed = (
        P("dp", None, "tensor"),
        P("tensor", None),
        P("dp", "tensor"),
        P("dp", "tensor"),
        P("dp", "tensor"),
    )
    return jax.shard_map(
        body,
        mesh=mesh,
        in_specs=placed,
        out_specs=(P("dp", "tensor"), P("dp", "tensor"), P("dp", "tensor")),
        check_vma=False,
    )
```

```python
import jax
import jax.numpy as jnp
from jax import lax
from jax.experimental import pallas as pl
from jax.experimental.pallas import tpu as pltpu
from jax.sharding import PartitionSpec as P

MESH = pl.DeviceIdType.MESH
F32, BF16 = jnp.float32, jnp.bfloat16

NX, NY, NZ, NZLO = 4, 8, 8, 4
ROWS, HALF, COLS, TILE = 48, 24, 512, 128
DEPTH = 1024
CHUNK = NY * ROWS

G_CORE, G_X, G_Y, G_YF, G_Z, G_M, G_D, G_P, G_S = 0, 4, 8, 12, 16, 17, 18, 19, 20
G_XF, G_GC, G_GX, G_GA, G_GB, GROUPS = 21, 22, 23, 24, 25, 26
GREET = 1
OWNER = (0, 1, 3, 2)
FAR = ((4, 3, 5, 6), (4, 5, 3, 2)) * 2
NEAR = ((2, 1, 7), (6, 7, 1)) * 2
BLOCKS = 4 * HALF
STRIPE = 64
PADDED = 32

CORE = [(0, 0, 0, 1)]


def hops(delta):
    return sum(min(d, n - d) for d, n in zip(delta, (NX, NY, NZ, 2)))


def farthest_first(deltas):
    return sorted(deltas, key=hops, reverse=True)


XS = farthest_first([(d, 0, 0, 0) for d in range(1, NX)])
YS = farthest_first([(0, d, 0, 0) for d in range(1, NY)])
ZS = farthest_first([(0, 0, d, 0) for d in range(1, NZ)])
XC = farthest_first([(d, 0, 0, k) for d in range(NX) for k in range(2) if (d, k) != (0, 0)])
YZ = farthest_first([(0, a, b, 0) for a in range(NY) for b in range(NZ) if (a, b) != (0, 0)])
HC = farthest_first([(0, 0, h, k) for h in (0, 4) for k in range(2) if (h, k) != (0, 0)])
PARTNERS = farthest_first(dict.fromkeys(YS + ZS + HC + XC))


def flip(block):
    rows, cols = block.shape
    wide = jnp.concatenate([block, jnp.zeros((rows, 128 - cols), F32)], axis=1)
    square = jnp.concatenate([wide, jnp.zeros((128 - rows, 128), F32)], axis=0)
    return square.T[:cols, :rows]


def kernel(
    grads, projector, first, second,
    step, mean_t,
    gbuf, pbuf, mom_t, mom, acc, crecv, xsend, xrecv, ysend, yrecv, zown, zrecv,
    yfsend, yfrecv, xfsum, xfsend, xfrecv, gram, gcsend, gcrecv, gsum, gxsend, gxrecv, gfull,
    mrecv, pboth, dsend, dall, upd, sown, sbox,
    lsem, send_sem, recv_sem,
):
    dp, tensor = lax.axis_index("dp"), lax.axis_index("tensor")
    zlo, y = dp // NY, dp % NY
    x, zhi, core = tensor // 4, (tensor // 2) % 2, tensor % 2
    z = zhi * NZLO + zlo
    other = 1 - core
    quarter = zhi * 2 + core

    def at(delta):
        dx, dy, dz, dk = delta
        px, py, pz, pk = (x + dx) % NX, (y + dy) % NY, (z + dz) % NZ, (core + dk) % 2
        return ((pz % NZLO) * NY + py, px * 4 + (pz // NZLO) * 2 + pk)

    started = {}

    def send(group, like, src, dst, delta):
        pltpu.make_async_remote_copy(
            src_ref=src, dst_ref=dst, send_sem=send_sem.at[group], recv_sem=recv_sem.at[group],
            device_id=at(delta), device_id_type=MESH,
        ).start()
        started[group] = like

    def arrived(group):
        like = started[group]
        pltpu.make_async_copy(like, like, recv_sem.at[group]).wait()

    def sent(groups):
        for group in groups:
            like = started[group]
            pltpu.make_async_copy(like, like, send_sem.at[group]).wait()

    loads = [pltpu.make_async_copy(projector, pbuf, lsem.at[0])]
    for s in range(NZLO):
        chunk = (zlo + OWNER[s]) % NZLO
        rows = pl.ds(pl.multiple_of(chunk * CHUNK, CHUNK), CHUNK)
        loads.append(pltpu.make_async_copy(grads.at[0, rows], gbuf.at[s], lsem.at[1 + s]))
    loads.append(pltpu.make_async_copy(first, mom_t.at[0], lsem.at[5]))
    loads.append(pltpu.make_async_copy(second, mom_t.at[1], lsem.at[6]))

    for load in loads[:2]:
        load.start()
    barrier = pltpu.get_barrier_semaphore()
    for delta in PARTNERS:
        pl.semaphore_signal(barrier, inc=1, device_id=at(delta), device_id_type=MESH)
    for load in loads[2:]:
        load.start()

    loads[0].wait()

    def core_send(s):
        send(G_CORE + s, crecv.at[s], acc.at[s, :, other], crecv.at[s], CORE[0])

    for s in range(NZLO):
        loads[1 + s].wait()
        out = jnp.dot(gbuf[s], pbuf[...], preferred_element_type=F32)
        acc[s] = out.reshape(NY, 2, HALF, COLS)
        if s == GREET:
            pl.semaphore_wait(barrier, len(PARTNERS))
            for t in range(s):
                core_send(t)
        if s >= GREET:
            core_send(s)

    def stacked(block):
        return jnp.concatenate([block[:, t * TILE:(t + 1) * TILE] for t in range(NX)], axis=0)

    def mine(s, d, lanes):
        there = (y + d) % NY
        return acc[s, there, core, :, lanes] + crecv[s, there, :, lanes]

    def along_x(s):
        for j, delta in enumerate(XS):
            lanes = pl.ds(pl.multiple_of(((x + delta[0]) % NX) * TILE, TILE), TILE)
            xsend[s, j] = jnp.concatenate([mine(s, d, lanes) for d in FAR[s]], axis=0).astype(BF16)
            send(G_X + s, xrecv.at[s], xsend.at[s, j], xrecv.at[s, j], delta)

    def along_y_first(s):
        for j, d in enumerate(NEAR[s]):
            yfsend[s, j] = stacked(mine(s, d, slice(None))).astype(BF16)
            send(G_YF + s, yfrecv.at[s], yfsend.at[s, j], yfrecv.at[s, j], (0, d, 0, 0))

    for s in range(NZLO):
        arrived(G_CORE + s)
        along_x(s)
        along_y_first(s)

    loads[5].wait()
    loads[6].wait()
    mom[0] = flip(mom_t[0])
    mom[1] = flip(mom_t[1])
    for j, delta in enumerate(HC):
        target_half = (core + delta[3]) % 2
        rows = pl.ds(pl.multiple_of(target_half * HALF, 8), HALF)
        send(G_M, mrecv.at[0:3], mom.at[:, rows], mrecv.at[quarter], delta)
    mrecv[quarter] = mom[:, pl.ds(pl.multiple_of(core * HALF, 8), HALF)]

    gram[...] = lax.dot_general(
        pbuf[...], pbuf[...], (((0,), (0,)), ((), ())), preferred_element_type=F32
    ).reshape(2, COLS // 2, COLS)
    gcsend[...] = gram[other].astype(BF16)
    send(G_GC, gcrecv, gcsend, gcrecv, CORE[0])

    def along_y(s):
        arrived(G_X + s)
        lanes = pl.ds(pl.multiple_of(x * TILE, TILE), TILE)
        others = xrecv[s, 0].astype(F32)
        for j in range(1, len(XS)):
            others = others + xrecv[s, j].astype(F32)
        for j, d in enumerate(FAR[s]):
            total = mine(s, d, lanes) + others[j * HALF:(j + 1) * HALF]
            padded = jnp.concatenate([total, jnp.zeros((PADDED - HALF, TILE), F32)], axis=0)
            ysend[s, j] = padded.astype(BF16)
            send(G_Y + s, yrecv.at[s], ysend.at[s, j], yrecv.at[s, j], (0, d, 0, 0))

    def gathered_along_y(s):
        arrived(G_YF + s)
        total = stacked(mine(s, 0, slice(None)))
        for j in range(len(NEAR[s])):
            total = total + yfrecv[s, j].astype(F32)
        xfsum[:, s] = total.reshape(NX, HALF, TILE)

    along_y(0)
    gathered_along_y(0)
    along_y(1)
    gathered_along_y(1)
    arrived(G_GC)
    gsum[...] = (gram[core] + gcrecv[...].astype(F32)).reshape(NX, STRIPE, COLS)
    for j, delta in enumerate(XS):
        gxsend[j] = gsum[(x + delta[0]) % NX].astype(BF16)
        send(G_GX, gxrecv, gxsend.at[j], gxrecv.at[j], delta)
    along_y(2)
    along_y(3)
    gathered_along_y(2)
    gathered_along_y(3)
    for j, delta in enumerate(XS):
        tile = xfsum[(x + delta[0]) % NX].reshape(BLOCKS, TILE)
        xfsend[j] = tile.astype(BF16)
        send(G_XF, xfrecv, xfsend.at[j], xfrecv.at[j], delta)

    arrived(G_XF)
    for s in range(NZLO):
        total = xfsum[x, s]
        for j in range(len(XS)):
            total = total + xfrecv[j].astype(F32)[s * HALF:(s + 1) * HALF]
        arrived(G_Y + s)
        for j in range(len(FAR[s])):
            total = total + yrecv[s, j, 0:HALF].astype(F32)
        zown[s] = total
        for d in (OWNER[s] + NZLO, OWNER[s]):
            if d > 0:
                send(G_Z, zrecv, zown.at[s], zrecv.at[d - 1], (0, 0, d, 0))

    stripe = gsum[x]
    arrived(G_GX)
    for j in range(len(XS)):
        stripe = stripe + gxrecv[j].astype(F32)
    gfull[core, x] = stripe.astype(BF16)
    for delta in XS:
        send(G_GA, gfull.at[core, 0:3], gfull.at[core, x], gfull.at[core, x], delta)

    arrived(G_M)
    m_first = jnp.concatenate([mrecv[q, 0] for q in range(4)], axis=1)
    m_second = jnp.concatenate([mrecv[q, 1] for q in range(4)], axis=1)
    total = zown[0]
    arrived(G_Z)
    for d in range(1, NZ):
        total = total + zrecv[d - 1]
    averaged = total * (1.0 / 32.0)

    def moments(old_first, old_second, mean):
        return 0.9 * old_first + 0.1 * mean, 0.999 * old_second + 0.001 * mean * mean

    f, v = moments(m_first, m_second, averaged)
    direction = f / (jnp.sqrt(v) + 1e-08)
    direction = jnp.concatenate([direction, jnp.zeros((8, TILE), F32)], axis=0).astype(BF16)
    dsend[...] = direction
    for delta in XC:
        send(G_D, dall.at[0:7], dsend, dall.at[core * NX + x], delta)
    pboth[core] = averaged
    send(G_P, pboth.at[core], pboth.at[core], pboth.at[core], CORE[0])
    dall[core * NX + x] = direction
    arrived(G_GA)
    send(G_GB, gfull.at[core], gfull.at[core], gfull.at[core], CORE[0])
    arrived(G_D)
    whole = jnp.concatenate(
        [jnp.concatenate([dall[k * NX + t] for t in range(NX)], axis=1) for k in range(2)], axis=0
    )
    arrived(G_GB)
    square = jnp.dot(whole, gfull[...].reshape(COLS, COLS), preferred_element_type=F32)
    square = square * whole.astype(F32)
    folded = square[0:8]
    for r in range(1, 8):
        folded = folded + square[8 * r:8 * r + 8]
    lanes_sum = folded[:, 0:TILE]
    for t in range(1, NX):
        lanes_sum = lanes_sum + folded[:, t * TILE:(t + 1) * TILE]
    total = jnp.sum(lanes_sum, axis=0, keepdims=True)

    sown[...] = total
    for j, delta in enumerate(YZ):
        send(G_S, sbox, sown, sbox.at[j], delta)
    update = lax.dot_general(
        whole, pbuf[...], (((1,), (1,)), ((), ())), preferred_element_type=F32
    )
    upd[...] = jnp.concatenate([update[0:HALF], update[32:32 + HALF]], axis=0)
    arrived(G_P)
    pieces = []
    for k in range(2):
        mean = pboth[k]
        piece = mean[:, 0:32]
        for q in range(1, 4):
            piece = jnp.where(quarter == q, mean[:, 32 * q:32 * q + 32], piece)
        pieces.append(piece)
    mean_t[...] = flip(jnp.concatenate(pieces, axis=0))
    sent(g for g in range(GROUPS) if g != G_S)
    arrived(G_S)
    total = total + jnp.sum(sbox[...], axis=0)

    total_sq = jnp.maximum(jnp.sum(total, axis=1, keepdims=True), 0.0)
    entries = float(1536 * 16384)
    factor = jnp.minimum(1.0, 0.02 * entries**0.5 / (jnp.sqrt(total_sq) + 1e-06))
    step[...] = factor * upd[...]
    sent((G_S,))


def body(grads, projector, weight, first_moment, second_moment):
    sem = pltpu.SemaphoreType.DMA
    vm = pltpu.VMEM
    operands = (grads, projector, first_moment.T, second_moment.T)
    step, mean_t = pl.pallas_call(
        kernel,
        name="galore_step",
        out_shape=(
            jax.ShapeDtypeStruct((ROWS, DEPTH), F32),
            jax.ShapeDtypeStruct((32, ROWS), F32),
        ),
        in_specs=[pl.BlockSpec(memory_space=pltpu.HBM)] * 4,
        out_specs=(pl.BlockSpec(memory_space=pltpu.VMEM),) * 2,
        scratch_shapes=[
            vm((NZLO, CHUNK, DEPTH), BF16),
            vm((DEPTH, COLS), BF16),
            vm((2, 32, ROWS), F32),
            vm((2, ROWS, 32), F32),
            vm((NZLO, NY, 2, HALF, COLS), F32),
            vm((NZLO, NY, HALF, COLS), F32),
            vm((NZLO, 3, BLOCKS, TILE), BF16),
            vm((NZLO, 3, BLOCKS, TILE), BF16),
            vm((NZLO, 4, PADDED, TILE), BF16),
            vm((NZLO, 4, PADDED, TILE), BF16),
            vm((NZLO, HALF, TILE), F32),
            vm((7, HALF, TILE), F32),
            vm((NZLO, 3, NX * HALF, TILE), BF16),
            vm((NZLO, 3, NX * HALF, TILE), BF16),
            vm((NX, NZLO, HALF, TILE), F32),
            vm((3, BLOCKS, TILE), BF16),
            vm((3, BLOCKS, TILE), BF16),
            vm((2, COLS // 2, COLS), F32),
            vm((COLS // 2, COLS), BF16),
            vm((COLS // 2, COLS), BF16),
            vm((NX, STRIPE, COLS), F32),
            vm((3, STRIPE, COLS), BF16),
            vm((3, STRIPE, COLS), BF16),
            vm((2, NX, STRIPE, COLS), BF16),
            vm((4, 2, HALF, 32), F32),
            vm((2, HALF, TILE), F32),
            vm((32, TILE), BF16),
            vm((2 * NX, 32, TILE), BF16),
            vm((ROWS, DEPTH), F32),
            vm((1, TILE), F32),
            vm((NY * NZ - 1, 1, TILE), F32),
            sem((7,)),
            sem((GROUPS,)),
            sem((GROUPS,)),
        ],
        compiler_params=pltpu.CompilerParams(
            collective_id=0, has_side_effects=True, vmem_limit_bytes=48 * 2**20
        ),
    )(*(pltpu.with_memory_space_constraint(a, pltpu.HBM) for a in operands))
    mean = mean_t.T
    new_first = 0.9 * first_moment + 0.1 * mean
    new_second = 0.999 * second_moment + 0.001 * mean * mean
    return weight - step, new_first, new_second


def solution(mesh):
    placed = (
        P("dp", None, "tensor"),
        P("tensor", None),
        P("dp", "tensor"),
        P("dp", "tensor"),
        P("dp", "tensor"),
    )
    return jax.shard_map(
        body,
        mesh=mesh,
        in_specs=placed,
        out_specs=(P("dp", "tensor"), P("dp", "tensor"), P("dp", "tensor")),
        check_vma=False,
    )
```

```python
import jax
import jax.numpy as jnp
from jax import lax
from jax.experimental import pallas as pl
from jax.experimental.pallas import tpu as pltpu
from jax.sharding import PartitionSpec as P

MESH = pl.DeviceIdType.MESH
F32, BF16 = jnp.float32, jnp.bfloat16

NX, NY, NZ, NZLO = 4, 8, 8, 4
ROWS, HALF, COLS, TILE = 48, 24, 512, 128
DEPTH = 1024
CHUNK = NY * ROWS

G_CORE, G_X, G_Y, G_YF, G_Z, G_M, G_D, G_P, G_S = 0, 4, 8, 12, 16, 17, 18, 19, 20
G_XF, G_GC, G_GX, G_GA, G_GB, GROUPS = 21, 23, 24, 25, 26, 27
GREET = 1
OWNER = (0, 1, 3, 2)
FAR = ((4, 3, 5, 6), (4, 5, 3, 2)) * 2
NEAR = ((2, 1, 7), (6, 7, 1)) * 2
BLOCKS = 4 * HALF
STRIPE = 64
PADDED = 32

CORE = [(0, 0, 0, 1)]


def hops(delta):
    return sum(min(d, n - d) for d, n in zip(delta, (NX, NY, NZ, 2)))


def farthest_first(deltas):
    return sorted(deltas, key=hops, reverse=True)


XS = farthest_first([(d, 0, 0, 0) for d in range(1, NX)])
YS = farthest_first([(0, d, 0, 0) for d in range(1, NY)])
ZS = farthest_first([(0, 0, d, 0) for d in range(1, NZ)])
XC = farthest_first([(d, 0, 0, k) for d in range(NX) for k in range(2) if (d, k) != (0, 0)])
YZ = farthest_first([(0, a, b, 0) for a in range(NY) for b in range(NZ) if (a, b) != (0, 0)])
HC = farthest_first([(0, 0, h, k) for h in (0, 4) for k in range(2) if (h, k) != (0, 0)])
PARTNERS = farthest_first(dict.fromkeys(YS + ZS + HC + XC))


def flip(block):
    rows, cols = block.shape
    wide = jnp.concatenate([block, jnp.zeros((rows, 128 - cols), F32)], axis=1)
    square = jnp.concatenate([wide, jnp.zeros((128 - rows, 128), F32)], axis=0)
    return square.T[:cols, :rows]


def kernel(
    grads, projector, first, second,
    step, mean_t,
    gbuf, pbuf, mom_t, mom, acc, crecv, xsend, xrecv, ysend, yrecv, zown, zrecv,
    yfsend, yfrecv, xfsum, xfsend, xfrecv, gram, gcsend, gcrecv, gsum, gxsend, gxrecv, gfull,
    mrecv, pboth, dsend, dall, upd, sown, sbox,
    lsem, send_sem, recv_sem,
):
    dp, tensor = lax.axis_index("dp"), lax.axis_index("tensor")
    zlo, y = dp // NY, dp % NY
    x, zhi, core = tensor // 4, (tensor // 2) % 2, tensor % 2
    z = zhi * NZLO + zlo
    other = 1 - core
    quarter = zhi * 2 + core

    def at(delta):
        dx, dy, dz, dk = delta
        px, py, pz, pk = (x + dx) % NX, (y + dy) % NY, (z + dz) % NZ, (core + dk) % 2
        return ((pz % NZLO) * NY + py, px * 4 + (pz // NZLO) * 2 + pk)

    started = {}

    def send(group, like, src, dst, delta):
        pltpu.make_async_remote_copy(
            src_ref=src, dst_ref=dst, send_sem=send_sem.at[group], recv_sem=recv_sem.at[group],
            device_id=at(delta), device_id_type=MESH,
        ).start()
        started[group] = like

    def arrived(group):
        like = started[group]
        pltpu.make_async_copy(like, like, recv_sem.at[group]).wait()

    def sent(groups):
        for group in groups:
            like = started[group]
            pltpu.make_async_copy(like, like, send_sem.at[group]).wait()

    loads = [pltpu.make_async_copy(projector, pbuf, lsem.at[0])]
    for s in range(NZLO):
        chunk = (zlo + OWNER[s]) % NZLO
        rows = pl.ds(pl.multiple_of(chunk * CHUNK, CHUNK), CHUNK)
        loads.append(pltpu.make_async_copy(grads.at[0, rows], gbuf.at[s], lsem.at[1 + s]))
    loads.append(pltpu.make_async_copy(first, mom_t.at[0], lsem.at[5]))
    loads.append(pltpu.make_async_copy(second, mom_t.at[1], lsem.at[6]))

    for load in loads[:2]:
        load.start()
    barrier = pltpu.get_barrier_semaphore()
    for delta in PARTNERS:
        pl.semaphore_signal(barrier, inc=1, device_id=at(delta), device_id_type=MESH)
    for load in loads[2:]:
        load.start()

    loads[0].wait()

    def core_send(s):
        send(G_CORE + s, crecv.at[s], acc.at[s, :, other], crecv.at[s], CORE[0])

    for s in range(NZLO):
        loads[1 + s].wait()
        out = jnp.dot(gbuf[s], pbuf[...], preferred_element_type=F32)
        acc[s] = out.reshape(NY, 2, HALF, COLS)
        if s == GREET:
            pl.semaphore_wait(barrier, len(PARTNERS))
            for t in range(s):
                core_send(t)
        if s >= GREET:
            core_send(s)

    def stacked(block):
        return jnp.concatenate([block[:, t * TILE:(t + 1) * TILE] for t in range(NX)], axis=0)

    def mine(s, d, lanes):
        there = (y + d) % NY
        return acc[s, there, core, :, lanes] + crecv[s, there, :, lanes]

    def along_x(s):
        for j, delta in enumerate(XS):
            lanes = pl.ds(pl.multiple_of(((x + delta[0]) % NX) * TILE, TILE), TILE)
            xsend[s, j] = jnp.concatenate([mine(s, d, lanes) for d in FAR[s]], axis=0).astype(BF16)
            send(G_X + s, xrecv.at[s], xsend.at[s, j], xrecv.at[s, j], delta)

    def along_y_first(s):
        for j, d in enumerate(NEAR[s]):
            yfsend[s, j] = stacked(mine(s, d, slice(None))).astype(BF16)
            send(G_YF + s, yfrecv.at[s], yfsend.at[s, j], yfrecv.at[s, j], (0, d, 0, 0))

    for s in range(NZLO):
        arrived(G_CORE + s)
        along_x(s)
        along_y_first(s)

    loads[5].wait()
    loads[6].wait()
    mom[0] = flip(mom_t[0])
    mom[1] = flip(mom_t[1])
    for j, delta in enumerate(HC):
        target_half = (core + delta[3]) % 2
        rows = pl.ds(pl.multiple_of(target_half * HALF, 8), HALF)
        send(G_M, mrecv.at[0:3], mom.at[:, rows], mrecv.at[quarter], delta)
    mrecv[quarter] = mom[:, pl.ds(pl.multiple_of(core * HALF, 8), HALF)]

    gram[...] = lax.dot_general(
        pbuf[...], pbuf[...], (((0,), (0,)), ((), ())), preferred_element_type=F32
    ).reshape(2, COLS // 2, COLS)
    gcsend[...] = gram[other].astype(BF16)
    send(G_GC, gcrecv, gcsend, gcrecv, CORE[0])

    def along_y(s):
        arrived(G_X + s)
        lanes = pl.ds(pl.multiple_of(x * TILE, TILE), TILE)
        others = xrecv[s, 0].astype(F32)
        for j in range(1, len(XS)):
            others = others + xrecv[s, j].astype(F32)
        for j, d in enumerate(FAR[s]):
            total = mine(s, d, lanes) + others[j * HALF:(j + 1) * HALF]
            padded = jnp.concatenate([total, jnp.zeros((PADDED - HALF, TILE), F32)], axis=0)
            ysend[s, j] = padded.astype(BF16)
            send(G_Y + s, yrecv.at[s], ysend.at[s, j], yrecv.at[s, j], (0, d, 0, 0))

    def gathered_along_y(s):
        arrived(G_YF + s)
        total = stacked(mine(s, 0, slice(None)))
        for j in range(len(NEAR[s])):
            total = total + yfrecv[s, j].astype(F32)
        xfsum[:, s] = total.reshape(NX, HALF, TILE)

    def along_x_after(half):
        for j, delta in enumerate(XS):
            tile = xfsum[(x + delta[0]) % NX, 2 * half:2 * half + 2].reshape(2 * HALF, TILE)
            xfsend[half, j] = tile.astype(BF16)
            send(G_XF + half, xfrecv.at[half], xfsend.at[half, j], xfrecv.at[half, j], delta)

    along_y(0)
    gathered_along_y(0)
    along_y(1)
    gathered_along_y(1)
    along_x_after(0)
    arrived(G_GC)
    gsum[...] = (gram[core] + gcrecv[...].astype(F32)).reshape(NX, STRIPE, COLS)
    for j, delta in enumerate(XS):
        gxsend[j] = gsum[(x + delta[0]) % NX].astype(BF16)
        send(G_GX, gxrecv, gxsend.at[j], gxrecv.at[j], delta)
    along_y(2)
    along_y(3)
    gathered_along_y(2)
    gathered_along_y(3)
    along_x_after(1)

    for s in range(NZLO):
        half, row = s // 2, s % 2 * HALF
        if s % 2 == 0:
            arrived(G_XF + half)
        total = xfsum[x, s]
        for j in range(len(XS)):
            total = total + xfrecv[half, j].astype(F32)[row:row + HALF]
        arrived(G_Y + s)
        for j in range(len(FAR[s])):
            total = total + yrecv[s, j, 0:HALF].astype(F32)
        zown[s] = total
        for d in (OWNER[s] + NZLO, OWNER[s]):
            if d > 0:
                send(G_Z, zrecv, zown.at[s], zrecv.at[d - 1], (0, 0, d, 0))

    stripe = gsum[x]
    arrived(G_GX)
    for j in range(len(XS)):
        stripe = stripe + gxrecv[j].astype(F32)
    gfull[core, x] = stripe.astype(BF16)
    for delta in XS:
        send(G_GA, gfull.at[core, 0:3], gfull.at[core, x], gfull.at[core, x], delta)

    arrived(G_M)
    m_first = jnp.concatenate([mrecv[q, 0] for q in range(4)], axis=1)
    m_second = jnp.concatenate([mrecv[q, 1] for q in range(4)], axis=1)
    total = zown[0]
    arrived(G_Z)
    for d in range(1, NZ):
        total = total + zrecv[d - 1]
    averaged = total * (1.0 / 32.0)

    def moments(old_first, old_second, mean):
        return 0.9 * old_first + 0.1 * mean, 0.999 * old_second + 0.001 * mean * mean

    f, v = moments(m_first, m_second, averaged)
    direction = f / (jnp.sqrt(v) + 1e-08)
    direction = jnp.concatenate([direction, jnp.zeros((8, TILE), F32)], axis=0).astype(BF16)
    dsend[...] = direction
    for delta in XC:
        send(G_D, dall.at[0:7], dsend, dall.at[core * NX + x], delta)
    pboth[core] = averaged
    send(G_P, pboth.at[core], pboth.at[core], pboth.at[core], CORE[0])
    dall[core * NX + x] = direction
    arrived(G_GA)
    send(G_GB, gfull.at[core], gfull.at[core], gfull.at[core], CORE[0])
    arrived(G_D)
    whole = jnp.concatenate(
        [jnp.concatenate([dall[k * NX + t] for t in range(NX)], axis=1) for k in range(2)], axis=0
    )
    arrived(G_GB)
    square = jnp.dot(whole, gfull[...].reshape(COLS, COLS), preferred_element_type=F32)
    square = square * whole.astype(F32)
    folded = square[0:8]
    for r in range(1, 8):
        folded = folded + square[8 * r:8 * r + 8]
    lanes_sum = folded[:, 0:TILE]
    for t in range(1, NX):
        lanes_sum = lanes_sum + folded[:, t * TILE:(t + 1) * TILE]
    total = jnp.sum(lanes_sum, axis=0, keepdims=True)

    sown[...] = total
    for j, delta in enumerate(YZ):
        send(G_S, sbox, sown, sbox.at[j], delta)
    update = lax.dot_general(
        whole, pbuf[...], (((1,), (1,)), ((), ())), preferred_element_type=F32
    )
    upd[...] = jnp.concatenate([update[0:HALF], update[32:32 + HALF]], axis=0)
    arrived(G_P)
    pieces = []
    for k in range(2):
        mean = pboth[k]
        piece = mean[:, 0:32]
        for q in range(1, 4):
            piece = jnp.where(quarter == q, mean[:, 32 * q:32 * q + 32], piece)
        pieces.append(piece)
    mean_t[...] = flip(jnp.concatenate(pieces, axis=0))
    sent(g for g in range(GROUPS) if g != G_S)
    arrived(G_S)
    total = total + jnp.sum(sbox[...], axis=0)

    total_sq = jnp.maximum(jnp.sum(total, axis=1, keepdims=True), 0.0)
    entries = float(1536 * 16384)
    factor = jnp.minimum(1.0, 0.02 * entries**0.5 / (jnp.sqrt(total_sq) + 1e-06))
    step[...] = factor * upd[...]
    sent((G_S,))


def body(grads, projector, weight, first_moment, second_moment):
    sem = pltpu.SemaphoreType.DMA
    vm = pltpu.VMEM
    operands = (grads, projector, first_moment.T, second_moment.T)
    step, mean_t = pl.pallas_call(
        kernel,
        name="galore_step",
        out_shape=(
            jax.ShapeDtypeStruct((ROWS, DEPTH), F32),
            jax.ShapeDtypeStruct((32, ROWS), F32),
        ),
        in_specs=[pl.BlockSpec(memory_space=pltpu.HBM)] * 4,
        out_specs=(pl.BlockSpec(memory_space=pltpu.VMEM),) * 2,
        scratch_shapes=[
            vm((NZLO, CHUNK, DEPTH), BF16),
            vm((DEPTH, COLS), BF16),
            vm((2, 32, ROWS), F32),
            vm((2, ROWS, 32), F32),
            vm((NZLO, NY, 2, HALF, COLS), F32),
            vm((NZLO, NY, HALF, COLS), F32),
            vm((NZLO, 3, BLOCKS, TILE), BF16),
            vm((NZLO, 3, BLOCKS, TILE), BF16),
            vm((NZLO, 4, PADDED, TILE), BF16),
            vm((NZLO, 4, PADDED, TILE), BF16),
            vm((NZLO, HALF, TILE), F32),
            vm((7, HALF, TILE), F32),
            vm((NZLO, 3, NX * HALF, TILE), BF16),
            vm((NZLO, 3, NX * HALF, TILE), BF16),
            vm((NX, NZLO, HALF, TILE), F32),
            vm((2, 3, 2 * HALF, TILE), BF16),
            vm((2, 3, 2 * HALF, TILE), BF16),
            vm((2, COLS // 2, COLS), F32),
            vm((COLS // 2, COLS), BF16),
            vm((COLS // 2, COLS), BF16),
            vm((NX, STRIPE, COLS), F32),
            vm((3, STRIPE, COLS), BF16),
            vm((3, STRIPE, COLS), BF16),
            vm((2, NX, STRIPE, COLS), BF16),
            vm((4, 2, HALF, 32), F32),
            vm((2, HALF, TILE), F32),
            vm((32, TILE), BF16),
            vm((2 * NX, 32, TILE), BF16),
            vm((ROWS, DEPTH), F32),
            vm((1, TILE), F32),
            vm((NY * NZ - 1, 1, TILE), F32),
            sem((7,)),
            sem((GROUPS,)),
            sem((GROUPS,)),
        ],
        compiler_params=pltpu.CompilerParams(
            collective_id=0, has_side_effects=True, vmem_limit_bytes=48 * 2**20
        ),
    )(*(pltpu.with_memory_space_constraint(a, pltpu.HBM) for a in operands))
    mean = mean_t.T
    new_first = 0.9 * first_moment + 0.1 * mean
    new_second = 0.999 * second_moment + 0.001 * mean * mean
    return weight - step, new_first, new_second


def solution(mesh):
    placed = (
        P("dp", None, "tensor"),
        P("tensor", None),
        P("dp", "tensor"),
        P("dp", "tensor"),
        P("dp", "tensor"),
    )
    return jax.shard_map(
        body,
        mesh=mesh,
        in_specs=placed,
        out_specs=(P("dp", "tensor"), P("dp", "tensor"), P("dp", "tensor")),
        check_vma=False,
    )
```
